32 devices in a mesh: groups: 2 (over x), seq: 16 (over z, y, core).
Axes of the slice: x: 2, y: 2, z: 4, core: 2. Of those that a mesh axis runs over, the one named last changes fastest.
Arguments:
- tokens: bfloat16 [4096, 3072], P(('groups', 'seq')), parts along dimension 0
- grad_out: bfloat16 [4096, 3072], P(('groups', 'seq')), parts along dimension 0, may hold values from -6 to 6
- event_type: int32 [4096, 1], P(('groups', 'seq')), parts along dimension 0, may hold values from 0 to 3; in each aligned block of 128 rows (0 to 127, 128 to 255, ...) at most 36 rows name the same one
- type_gain: float32 [4, 3072], replicated, may hold values from 0.1 to 1.9
- up_weight: bfloat16 [3072, 24576], P(None, 'seq'), may hold values from -0.109375 to 0.109375
- down_weight: bfloat16 [24576, 3072], P('seq'), may hold values from -0.078125 to 0.078125
Outputs:
- grad_tokens: bfloat16 [4096, 3072], P(('groups', 'seq')), parts along dimension 0
- grad_gain: float32 [8, 3072], P('groups'), parts along dimension 0
- grad_up: bfloat16 [6144, 24576], P('groups', 'seq'), parts along dimension 0
- grad_down: bfloat16 [49152, 3072], P(('groups', 'seq')), parts along dimension 0
The draws below stay inside these ranges and needn't reach their ends.
There are 2 independent parts, one for each index of `groups`. The reference program is written for one: setup_inputs(seed, part) draws one part's arguments, and reference() takes and returns one part's arrays. A program takes and returns all parts, laid end to end along the dimension named above; an argument that names none is the same for every part. Nothing has to cross between parts.
Inputs may be any that keep to these rules, and one draw needn't show every extreme that they name: `event_type`: among the events of one index of seq, at most 36 have the same type, and some index reaches 36 in every draw.
All inputs are finite; a program needn't handle non-finite values.
Results may differ from the reference program's by a relative error of at most 0.006.
Values may be sent and summed in bfloat16 or wider, within the bound.
No kernel may reach another device: no remote copies, remote signals or barrier semaphores. Data moves between devices by JAX's collectives and lax.ppermute only.
A program may use at most 128 MiB of HBM per device.

```python
import math
import jax
import jax.numpy as jnp
import numpy as np
from jax import lax

D = 3072
FFW = 6144
TYPES = 4
TOK_DEV = 128
CAP = 36
TOKENS = 2048
N_SEQ = 16


def draw_tokens(key, part):
    key = jax.random.fold_in(key, 11)
    key_vals, key_cols, key_rows = jax.random.split(key, 3)
    col_scale = jnp.exp(jax.random.uniform(key_cols, (D,), jnp.float32, 0.0, math.log(10.0)))
    row_scale = jnp.exp(jax.random.uniform(key_rows, (TOKENS, 1), jnp.float32, 0.0, math.log(3.0)))
    values = jax.random.normal(key_vals, (TOKENS, D), jnp.float32)
    values = jnp.clip(values, -5.0, 5.0)
    return (values * col_scale[None, :] * row_scale / 4.6).astype(jnp.bfloat16)


def shard_levels(key, extent, shards, least, high):
    gain, own = 1.0, jax.random.fold_in(key, 6)
    for position, blocks in shards:
        heights = jnp.exp(jax.random.uniform(jax.random.fold_in(own, position), (blocks,), jnp.float32, least / len(shards), high / len(shards)))
        gain = gain * jnp.repeat(heights, extent[position] // blocks).reshape([-1 if axis == position else 1 for axis in range(len(extent))])
    return gain


def shared_out(key, own, number, rows, count, top, reach, skew):
    order = jax.random.permutation(key, count)
    heavy_load, common = portions_of(count, rows * top, reach, skew, True), portions_of(count, rows * top, reach, skew, False)
    places = jnp.arange(count)

    def named(lengths, offset_by):
        used = int((lengths > 0).sum())
        fixed = max(1, used // 4)
        passed = fixed + (places - fixed + offset_by * (used - fixed)) % max(1, count - fixed)
        return jnp.zeros((count,), jnp.int32).at[order[jnp.where(places < fixed, places, passed)]].set(jnp.asarray(lengths, jnp.int32))

    lengths = jnp.where(number % 4 == 0, named(heavy_load, number // 4), named(common, number - number // 4 - 1))
    mixed = jax.random.permutation(jax.random.fold_in(own, 3), count)
    donor, receiver = mixed[0:count // 2 * 2:2], mixed[1:count // 2 * 2:2]
    slack = jnp.minimum(lengths[donor] - 1, reach - lengths[receiver]) // 2
    slack = jnp.where((donor == order[0]) | (receiver == order[0]) | (lengths[receiver] == 0), 0, jnp.maximum(slack, 0))
    passed = jax.random.randint(jax.random.fold_in(own, 4), (count // 2,), 0, 1 << 20) % (slack + 1)
    lengths = lengths.at[donor].add(-passed).at[receiver].add(passed)
    labels = jnp.searchsorted(jnp.cumsum(lengths), jnp.arange(rows * top), side="right").astype(jnp.int32)
    table = labels.reshape(top, rows).T
    table = table[jax.random.permutation(jax.random.fold_in(own, 1), rows)]
    offset_by = jax.random.randint(jax.random.fold_in(own, 2), (rows, 1), 0, top)
    return jnp.take_along_axis(table, (jnp.arange(top)[None, :] + offset_by) % top, axis=1)


def portions_of(amount, total, most, lean, full):
    portions = [(1 << 20) // math.isqrt(rank ** lean) + 1 for rank in range(1, amount + 1)]
    largest = most if full else min(most, max(-(-total // amount), total * portions[0] // sum(portions)))
    least = 1 if total - largest >= amount - 1 else 0
    holding, spare = [largest] + [least] * (amount - 1), total - largest - least * (amount - 1)
    while spare > 0:
        free = [i for i in range(1, amount) if holding[i] < largest] or [i for i in range(1, amount) if holding[i] < most]
        pool, remaining = sum([portions[i] for i in free]), spare
        for i in free:
            more = min(most - holding[i], max(1, remaining * portions[i] // pool), spare)
            holding[i] = holding[i] + more
            spare = spare - more
    return np.array(holding)


def centred(stream_key, extent, spread, reach, pieces=(), kind=jnp.bfloat16):
    result = spread * jax.random.normal(stream_key, extent, jnp.float32)
    if pieces:
        result = result * shard_levels(stream_key, extent, pieces, -0.22, 0.18)
    return jnp.clip(result, -reach, reach).astype(kind)


def setup_inputs(seed: int = 0, part: int = 0) -> dict:
    splits = jax.random.split(jax.random.key(seed), 7)
    part_keys = jax.random.split(jax.random.fold_in(splits[6], part), 7)
    tokens = draw_tokens(jax.random.fold_in(jax.random.fold_in(splits[6], part), 71), part)
    grad_out = centred(part_keys[1], (TOKENS, D), 1.0, 6.0, ((0, 16),))
    event_type_keys = jax.random.split(jax.random.fold_in(part_keys[2], 1), TOKENS // TOK_DEV)
    event_type_turns = jax.random.permutation(jax.random.fold_in(part_keys[2], 3), TOKENS // TOK_DEV)
    event_type = jax.vmap(lambda own, number: shared_out(jax.random.fold_in(part_keys[2], 2), own, number, TOK_DEV, TYPES, 1, CAP, 2))(event_type_keys, event_type_turns).reshape((TOKENS, 1))
    type_gain = jnp.clip(1.0 + 0.18 * jax.random.normal(splits[3], (TYPES, D), jnp.float32), 0.1, 1.9)
    up_weight = centred(splits[4], (D, TYPES * FFW), D ** -0.5, 0.109375, ((1, 16),))
    down_weight = centred(splits[5], (TYPES * FFW, D), FFW ** -0.5, 0.078125, ((0, 16),))
    return {"tokens": tokens, "grad_out": grad_out, "event_type": event_type, "type_gain": type_gain, "up_weight": up_weight, "down_weight": down_weight}


EPS = 1e-06

def silu_parts(preact):
    gate_sig = jax.nn.sigmoid(preact)
    return (preact * gate_sig, gate_sig * (1.0 + preact * (1.0 - gate_sig)))

def reference(tokens, grad_out, event_type, type_gain, up_weight, down_weight):
    type_ids = event_type[:, 0].astype(jnp.int32)
    onehot = (type_ids[:, None] == jnp.arange(TYPES, dtype=jnp.int32)[None, :]).astype(jnp.int32)
    blocks = onehot.reshape(N_SEQ, TOK_DEV, TYPES)
    running = jnp.cumsum(blocks, axis=1) - 1
    slot_rank = lax.optimization_barrier(jnp.sum(running * blocks, axis=2)).reshape(-1).astype(jnp.int32)
    device = (jnp.arange(TOKENS, dtype=jnp.int32) // TOK_DEV).astype(jnp.int32)
    slot_index = (device * (TYPES * CAP) + type_ids * CAP + slot_rank).astype(jnp.int32)
    tok_f32 = tokens.astype(jnp.float32)
    inverse = lax.rsqrt(lax.optimization_barrier(jnp.mean(tok_f32 * tok_f32, axis=1, keepdims=True)) + EPS)
    gain_rows = type_gain[type_ids]
    normed = (tok_f32 * inverse * gain_rows).astype(jnp.bfloat16)
    packed_normed = jnp.zeros((N_SEQ * TYPES * CAP, D), jnp.bfloat16).at[slot_index].set(normed)
    packed_grad = jnp.zeros((N_SEQ * TYPES * CAP, D), jnp.bfloat16).at[slot_index].set(grad_out)
    packed_normed = packed_normed.reshape(N_SEQ, TYPES, CAP, D)
    packed_grad = packed_grad.reshape(N_SEQ, TYPES, CAP, D)
    owners = N_SEQ // TYPES
    hid_block = FFW // owners
    grads_up = []
    grads_down = []
    returned = []
    for kind in range(TYPES):
        rows_normed = packed_normed[:, kind].reshape(-1, D)
        rows_grad = packed_grad[:, kind].reshape(-1, D)
        up_kind = up_weight[:, kind * FFW:(kind + 1) * FFW]
        down_kind = down_weight[kind * FFW:(kind + 1) * FFW, :]
        preact = jnp.dot(rows_normed, up_kind, preferred_element_type=jnp.float32)
        act_f32, slope_term = silu_parts(preact)
        activation = act_f32.astype(jnp.bfloat16)
        grad_act = jnp.dot(rows_grad, down_kind.T, preferred_element_type=jnp.float32)
        grad_pre = (grad_act * slope_term).astype(jnp.bfloat16)
        total = jnp.zeros((rows_normed.shape[0], D), jnp.float32)
        for owner in range(owners):
            lower = owner * hid_block
            upper = lower + hid_block
            part_dx = jnp.dot(grad_pre[:, lower:upper], up_kind[:, lower:upper].T, preferred_element_type=jnp.float32)
            total = total + part_dx.astype(jnp.bfloat16).astype(jnp.float32)
        returned.append(total.reshape(N_SEQ, CAP, D))
        grads_up.append(jnp.dot(rows_normed.T, grad_pre, preferred_element_type=jnp.float32).astype(jnp.bfloat16))
        grads_down.append(jnp.dot(activation.T, rows_grad, preferred_element_type=jnp.float32).astype(jnp.bfloat16))
    returned_all = jnp.stack(returned, axis=1).reshape(-1, D)
    grad_normed = returned_all[slot_index]
    scaled = grad_normed * gain_rows
    inner_sum = lax.optimization_barrier(jnp.sum(scaled * tok_f32, axis=1, keepdims=True))
    branch = scaled * inverse - tok_f32 * inner_sum * inverse * inverse * inverse / D
    grad_tokens = (grad_out.astype(jnp.float32) + branch).astype(jnp.bfloat16)
    grad_gain = jnp.dot(onehot.astype(jnp.float32).T, grad_normed * tok_f32 * inverse, precision=lax.Precision.HIGHEST, preferred_element_type=jnp.float32)
    grad_up = jnp.concatenate(grads_up, axis=1)
    grad_down = jnp.concatenate(grads_down, axis=0)
    return (grad_tokens, grad_gain, grad_up, grad_down)
```

```python
import functools

import jax
import jax.numpy as jnp
from jax import lax
from jax.experimental import pallas as pl
from jax.experimental.pallas import tpu as pltpu
from jax.sharding import PartitionSpec as P

TYPES = 4
CAP = 36
MAIN = 32
TAIL = CAP - MAIN
BLOCK = 2 * CAP
EPS = 1e-06
CORES = 2

GROUPS = ((0, 1), (2,), (3,))

F32 = jnp.float32
BF16 = jnp.bfloat16
VMEM_LIMIT = 56 << 20
NT = (((1,), (1,)), ((), ()))
TN = (((0,), (0,)), ((), ()))


def params(limit=VMEM_LIMIT):
    return pltpu.CompilerParams(vmem_limit_bytes=limit)


def cost(flops, moved):
    return pl.CostEstimate(flops=int(flops), bytes_accessed=int(moved), transcendentals=0)


def token_terms(tokens_ref, type_ref, gain_ref):
    tok = tokens_ref[...].astype(F32)
    inverse = lax.rsqrt(jnp.mean(tok * tok, axis=1, keepdims=True) + EPS)
    types = type_ref[...]
    gain_rows = jnp.zeros_like(tok)
    for k in range(TYPES):
        gain_rows = jnp.where(types == k, gain_ref[k : k + 1, :], gain_rows)
    rows = tok.shape[0]
    lanes = lax.broadcasted_iota(jnp.int32, (rows, 128), 1)
    onehot = jnp.where(lanes == types, 1.0, 0.0)
    below = lax.broadcasted_iota(jnp.int32, (rows, rows), 1)
    above = lax.broadcasted_iota(jnp.int32, (rows, rows), 0)
    earlier = jnp.where(below < above, 1.0, 0.0).astype(BF16)
    running = jnp.dot(earlier, onehot.astype(BF16), preferred_element_type=F32)
    rank = jnp.sum(running * onehot, axis=1, keepdims=True).astype(jnp.int32)
    return tok, inverse, types, gain_rows, rank


def wide_mod(value):
    return jnp.where(value >= TYPES, value - TYPES, value)


def pack_kernel(plane_ref, tokens_ref, grad_ref, type_ref, gain_ref, *outs):
    tok, inverse, types, gain_rows, rank = token_terms(tokens_ref, type_ref, gain_ref)
    normed = (tok * inverse * gain_rows).astype(BF16)
    both = jnp.concatenate([normed, grad_ref[...]], axis=0)
    rows = tok.shape[0]
    lane = lax.broadcasted_iota(jnp.int32, (rows, BLOCK), 1)
    tail_n = lane - MAIN
    tail_g = lane - CAP
    slot_n = jnp.where(lane < MAIN, lane, jnp.where((lane >= 2 * MAIN) & (tail_n < CAP), tail_n, -1))
    slot_g = jnp.where((lane >= MAIN) & (lane < 2 * MAIN), lane - MAIN, jnp.where(tail_g >= MAIN, tail_g, -1))
    for shift, out in enumerate(outs):
        kind = wide_mod(plane_ref[0] + shift)
        here = types == kind
        pick_n = jnp.where(here & (rank == slot_n), 1.0, 0.0)
        pick_g = jnp.where(here & (rank == slot_g), 1.0, 0.0)
        pick = jnp.concatenate([pick_n, pick_g], axis=0).astype(BF16)
        out[...] = lax.dot_general(pick, both, TN, preferred_element_type=F32).astype(BF16)


def finish_kernel(plane_ref, tokens_ref, grad_ref, type_ref, gain_ref, *refs):
    returned = refs[:TYPES]
    gains = refs[TYPES : 2 * TYPES]
    out, gain_out = refs[2 * TYPES :]
    tok, inverse, types, gain_rows, rank = token_terms(tokens_ref, type_ref, gain_ref)
    rows, width = tok.shape
    lane = lax.broadcasted_iota(jnp.int32, (rows, BLOCK), 1)
    in_tail = lane >= 2 * MAIN
    slot_l = jnp.where(lane < MAIN, lane, jnp.where(in_tail & (lane < 2 * MAIN + TAIL), lane - MAIN, -1))
    slot_r = jnp.where(
        (lane >= MAIN) & ~in_tail, lane - MAIN, jnp.where(lane >= 2 * MAIN + TAIL, lane - CAP, -1)
    )
    left = jnp.zeros((rows, width // 2), F32)
    right = jnp.zeros((rows, width // 2), F32)
    for shift in range(TYPES):
        here = types == wide_mod(plane_ref[0] + shift)
        block = returned[shift][...]
        pick_l = jnp.where(here & (rank == slot_l), 1.0, 0.0).astype(BF16)
        pick_r = jnp.where(here & (rank == slot_r), 1.0, 0.0).astype(BF16)
        left += jnp.dot(pick_l, block, preferred_element_type=F32)
        right += jnp.dot(pick_r, block, preferred_element_type=F32)
    scaled = jnp.concatenate([left, right], axis=1) * gain_rows
    inner = jnp.sum(scaled * tok, axis=1, keepdims=True)
    branch = scaled * inverse - tok * (inner * inverse * inverse * inverse / width)
    out[...] = (grad_ref[...].astype(F32) + branch).astype(BF16)
    row = lax.broadcasted_iota(jnp.int32, (TYPES, width), 0)
    total = jnp.zeros((TYPES, width), F32)
    for shift in range(TYPES):
        kind = wide_mod(plane_ref[0] + TYPES - shift)
        total = jnp.where(row == kind, gains[shift][...], total)
    gain_out[...] = total / gain_ref[...]


def chunk_kernel(shifts, pairs, tile, out_tile, *refs):
    blocks = 2 * pairs * shifts
    ins = refs[:blocks]
    up, down, keep, send, normed, grads, act, pre, gain = refs[blocks : blocks + 9]
    blk, up_v, down_v, n_v, g_v, act_v, pre_v, keep_v, send_v, gain_v, in_sem, w_sem, o_sem = refs[blocks + 9 :]
    width, hidden = up.shape
    tiles = hidden // tile
    half = blocks // 2
    in_copies = [pltpu.make_async_copy(ins[i], blk.at[i], in_sem.at[i]) for i in range(blocks)]
    for copy in in_copies:
        copy.start()

    def up_copy(t):
        cols = pl.ds(pl.multiple_of(t * tile, tile), tile)
        return pltpu.make_async_copy(up.at[:, cols], up_v.at[:, cols], w_sem.at[0, t])

    def down_copy(t):
        rows = pl.ds(pl.multiple_of(t * tile, tile), tile)
        return pltpu.make_async_copy(down.at[rows, :], down_v.at[rows, :], w_sem.at[1, t])

    for t in range(tiles):
        up_copy(t).start()
        down_copy(t).start()
    for copy in in_copies:
        copy.wait()
    low = lax.broadcasted_iota(jnp.int32, (8, width), 0) < TAIL
    tails_n, tails_g = [], []
    for i in range(blocks):
        n_v[i * MAIN : (i + 1) * MAIN, :] = blk[i, 0:MAIN, :]
        g_v[i * MAIN : (i + 1) * MAIN, :] = blk[i, MAIN : 2 * MAIN, :]
    for i in range(0, blocks, 2):
        a = blk[i, 2 * MAIN : BLOCK, :].astype(F32)
        b = blk[i + 1, 2 * MAIN : BLOCK, :].astype(F32)
        tails_n.append(jnp.where(low, a, pltpu.roll(b, TAIL, 0)))
        tails_g.append(jnp.where(low, pltpu.roll(a, TAIL, 0), b))
    n_v[blocks * MAIN :, :] = jnp.concatenate(tails_n, axis=0).astype(BF16)
    g_v[blocks * MAIN :, :] = jnp.concatenate(tails_g, axis=0).astype(BF16)
    n_copy = pltpu.make_async_copy(n_v, normed, o_sem.at[0])
    g_copy = pltpu.make_async_copy(g_v, grads, o_sem.at[1])
    n_copy.start()
    g_copy.start()

    def forward(t, carry):
        cols = pl.ds(pl.multiple_of(t * tile, tile), tile)
        up_copy(t).wait()
        preact = jnp.dot(n_v[...], up_v[:, cols], preferred_element_type=F32)
        down_copy(t).wait()
        grad_act = lax.dot_general(g_v[...], down_v[cols, :], NT, preferred_element_type=F32)
        sig = jax.nn.sigmoid(preact)
        act_v[:, cols] = (preact * sig).astype(BF16)
        pre_v[:, cols] = (grad_act * (sig * (1.0 + preact * (1.0 - sig)))).astype(BF16)
        return carry

    lax.fori_loop(0, tiles, forward, 0)
    act_copy = pltpu.make_async_copy(act_v, act, o_sem.at[2])
    pre_copy = pltpu.make_async_copy(pre_v, pre, o_sem.at[3])
    act_copy.start()
    pre_copy.start()
    m, t4 = half * MAIN, half * TAIL

    def backward(t, carry):
        cols = pl.ds(pl.multiple_of(t * out_tile, out_tile), out_tile)
        dx = lax.dot_general(pre_v[...], up_v[cols, :], NT, preferred_element_type=F32)
        keep_v[0:m, cols] = dx[0:m]
        keep_v[m:, cols] = dx[2 * m : 2 * m + t4]
        send_v[:, cols] = jnp.concatenate([dx[m : 2 * m], dx[2 * m + t4 :]], axis=0).astype(BF16)
        gain_v[:, cols] = jnp.sum(dx * n_v[:, cols].astype(F32), axis=0, keepdims=True)
        return carry

    lax.fori_loop(0, width // out_tile, backward, 0)
    last = [
        pltpu.make_async_copy(send_v, send, o_sem.at[4]),
        pltpu.make_async_copy(keep_v, keep, o_sem.at[5]),
        pltpu.make_async_copy(gain_v, gain, o_sem.at[6]),
    ]
    for copy in last:
        copy.start()
    for copy in [n_copy, g_copy, act_copy, pre_copy] + last:
        copy.wait()


def run_chunk(blocks, up, down, shifts, pairs):
    width, hidden = up.shape
    rows = len(blocks) * CAP
    tile = min(512, hidden)
    out_tile = min(512, width)
    any_spec = pl.BlockSpec(memory_space=pl.ANY)
    shapes = [
        ((rows // 2, width), F32),
        ((rows // 2, width), BF16),
        ((rows, width), BF16),
        ((rows, width), BF16),
        ((rows, hidden), BF16),
        ((rows, hidden), BF16),
        ((1, width), F32),
    ]
    return pl.pallas_call(
        functools.partial(chunk_kernel, shifts, pairs, tile, out_tile),
        in_specs=[any_spec] * (len(blocks) + 2),
        out_specs=[any_spec] * len(shapes),
        out_shape=[jax.ShapeDtypeStruct(s, d) for s, d in shapes],
        scratch_shapes=[
            pltpu.VMEM((len(blocks), BLOCK, width), BF16),
            pltpu.VMEM((width, hidden), BF16),
            pltpu.VMEM((hidden, width), BF16),
            pltpu.VMEM((rows, width), BF16),
            pltpu.VMEM((rows, width), BF16),
            pltpu.VMEM((rows, hidden), BF16),
            pltpu.VMEM((rows, hidden), BF16),
            pltpu.VMEM((rows // 2, width), F32),
            pltpu.VMEM((rows // 2, width), BF16),
            pltpu.VMEM((1, width), F32),
            pltpu.SemaphoreType.DMA((len(blocks),)),
            pltpu.SemaphoreType.DMA((2, hidden // tile)),
            pltpu.SemaphoreType.DMA((7,)),
        ],
        compiler_params=params(),
        cost_estimate=cost(6 * rows * width * hidden, 4 * width * hidden),
    )(*blocks, up, down)


def split_kernel(shifts, pairs, keep_ref, recv_ref, *outs):
    half = keep_ref.shape[1] // 2
    low = lax.broadcasted_iota(jnp.int32, (8, half), 0) < TAIL
    base = shifts * pairs * MAIN
    for s in range(shifts):
        for i in range(pairs):
            at = s * pairs + i
            main = keep_ref[at * MAIN : (at + 1) * MAIN, :] + recv_ref[at * MAIN : (at + 1) * MAIN, :].astype(F32)
            first = base + (at // 2) * 8
            tail = keep_ref[first : first + 8, :] + recv_ref[first : first + 8, :].astype(F32)
            if at % 2 == 0:
                joined = jnp.where(low, tail[:, :half], pltpu.roll(tail[:, half:], TAIL, 0))
            else:
                joined = jnp.where(low, pltpu.roll(tail[:, :half], TAIL, 0), tail[:, half:])
            whole = jnp.concatenate([main[:, :half], main[:, half:], joined], axis=0)
            outs[i][s * BLOCK : (s + 1) * BLOCK, :] = whole.astype(outs[i].dtype)


def split_sum(keep, recv, shifts, pairs):
    width = keep.shape[1]
    shape = (shifts * BLOCK, width // 2)
    return pl.pallas_call(
        functools.partial(split_kernel, shifts, pairs),
        out_shape=[jax.ShapeDtypeStruct(shape, F32 if i == 0 else BF16) for i in range(pairs)],
        compiler_params=params(),
    )(keep, recv)


def weight_kernel(count, tile, *refs):
    lefts, rights, out = refs[:count], refs[count : 2 * count], refs[2 * count]
    stacked = refs[2 * count + 1]

    @pl.when(pl.program_id(0) == 0)
    def _():
        first = 0
        for right in rights:
            stacked[first : first + right.shape[0], :] = right[...]
            first += right.shape[0]

    left = jnp.concatenate([ref[...] for ref in lefts], axis=0)
    out[...] = lax.dot_general(left, stacked[...], TN, preferred_element_type=F32).astype(BF16)


def weight_grad(lefts, rights):
    rows = sum(x.shape[0] for x in lefts)
    long, wide = lefts[0].shape[1], rights[0].shape[1]
    tile = min(512, long)
    return pl.pallas_call(
        functools.partial(weight_kernel, len(lefts), tile),
        grid=(long // tile,),
        in_specs=[pl.BlockSpec((x.shape[0], tile), lambda j: (0, j)) for x in lefts]
        + [pl.BlockSpec(x.shape, lambda j: (0, 0)) for x in rights],
        out_specs=pl.BlockSpec((tile, wide), lambda j: (j, 0)),
        out_shape=jax.ShapeDtypeStruct((long, wide), BF16),
        scratch_shapes=[pltpu.VMEM((rows, wide), BF16)],
        compiler_params=params(),
        cost_estimate=cost(2 * rows * long * wide, 2 * long * wide),
    )(*lefts, *rights)


def local(tokens, grad_out, event_type, type_gain, up_weight, down_weight):
    seq = lax.axis_size("seq")
    owners = seq // TYPES
    pairs = owners // CORES
    width = tokens.shape[1]
    plane = (lax.axis_index("seq") // owners).astype(jnp.int32).reshape(1)

    def moved(x, to):
        return lax.ppermute(x, "seq", [(i, to(i)) for i in range(seq)])

    def to_plane(x, shift):
        return moved(x, lambda i: (i + shift * owners) % seq)

    def to_pair(x, shift):
        return moved(x, lambda i: i // owners * owners + (i % owners + CORES * shift) % owners)

    def to_core(x):
        return moved(x, lambda i: i ^ 1)

    smem = pl.BlockSpec(memory_space=pltpu.SMEM)
    vmem = pl.BlockSpec(memory_space=pltpu.VMEM)
    packed = pl.pallas_call(
        pack_kernel,
        in_specs=[smem] + [vmem] * 4,
        out_shape=[jax.ShapeDtypeStruct((BLOCK, width), BF16)] * TYPES,
        compiler_params=params(),
    )(plane, tokens, grad_out, event_type, type_gain)

    blocks = {}
    for shift in range(TYPES):
        own = to_plane(packed[shift], shift) if shift else packed[shift]
        mine = [own] + [to_pair(own, j) for j in range(1, pairs)]
        blocks[shift] = (mine, [to_core(x) for x in mine])

    acts, pres, norms, grads, returned = [], [], [], [], [None] * TYPES
    gain = jnp.zeros((1, width), F32)
    for group in GROUPS:
        order = [x for part in (0, 1) for shift in group for x in blocks[shift][part]]
        keep, send, normed, grad, act, pre, gain_part = run_chunk(
            order, up_weight, down_weight, len(group), pairs
        )
        acts.append(act)
        pres.append(pre)
        norms.append(normed)
        grads.append(grad)
        gain = gain + gain_part
        parts = split_sum(keep, to_core(send), len(group), pairs)
        total = parts[0]
        for j in range(1, pairs):
            total = total + to_pair(parts[j], pairs - j).astype(F32)
        for at, shift in enumerate(group):
            back = total[at * BLOCK : (at + 1) * BLOCK].astype(BF16)
            returned[shift] = to_plane(back, TYPES - shift) if shift else back

    gain = gain + to_core(gain)
    plane_gain = gain
    for j in range(1, pairs):
        plane_gain = plane_gain + to_pair(gain, j)
    gains = [plane_gain] + [to_plane(plane_gain, shift) for shift in range(1, TYPES)]

    grad_up = weight_grad(norms, pres)
    grad_down = weight_grad(acts, grads)
    grad_tokens, grad_gain = pl.pallas_call(
        finish_kernel,
        in_specs=[smem] + [vmem] * (4 + 2 * TYPES),
        out_shape=[
            jax.ShapeDtypeStruct(tokens.shape, BF16),
            jax.ShapeDtypeStruct((TYPES, width), F32),
        ],
        compiler_params=params(),
    )(plane, tokens, grad_out, event_type, type_gain, *returned, *gains)
    return (grad_tokens, grad_gain, grad_up, grad_down)


def solution(mesh):
    placed = (
        P(("groups", "seq"), None),
        P(("groups", "seq"), None),
        P(("groups", "seq"), None),
        P(),
        P(None, "seq"),
        P("seq", None),
    )
    return jax.shard_map(
        local,
        mesh=mesh,
        in_specs=placed,
        out_specs=(
            P(("groups", "seq"), None),
            P("groups", None),
            P("groups", "seq"),
            P(("groups", "seq"), None),
        ),
        check_vma=False,
    )
```

```python
import functools

import jax
import jax.numpy as jnp
from jax import lax
from jax.experimental import pallas as pl
from jax.experimental.pallas import tpu as pltpu
from jax.sharding import PartitionSpec as P

TYPES = 4
CAP = 36
MAIN = 32
TAIL = CAP - MAIN
HALF = 2 * CAP
PAIR = 2 * HALF
EPS = 1e-06
CORES = 2

F32 = jnp.float32
BF16 = jnp.bfloat16
VMEM_LIMIT = 8 << 20
FORWARD_TILE = 512
HASTE = 100000
TILES_FIRST = 2
NT = (((1,), (1,)), ((), ()))
TN = (((0,), (0,)), ((), ()))
HBM = pl.BlockSpec(memory_space=pltpu.HBM)
VMEM = pl.BlockSpec(memory_space=pltpu.VMEM)
SMEM = pl.BlockSpec(memory_space=pltpu.SMEM)


def params(rows=0):
    return pltpu.CompilerParams(vmem_limit_bytes=VMEM_LIMIT + rows * 40 * 1024)


def cost(flops, moved):
    return pl.CostEstimate(flops=int(flops) // HASTE, bytes_accessed=int(moved) // HASTE, transcendentals=0)


def sum_kernel(count, *refs):
    refs[-1][...] = sum(ref[...] for ref in refs[:count])


def summed(parts, after):
    return pl.pallas_call(
        functools.partial(sum_kernel, len(parts)),
        in_specs=[VMEM] * len(parts) + [HBM] * len(after),
        out_specs=VMEM,
        out_shape=jax.ShapeDtypeStruct(parts[0].shape, F32),
        compiler_params=params(),
    )(*parts, *after)


def token_terms(tokens_ref, type_ref, gain_ref):
    tok = tokens_ref[...].astype(F32)
    inverse = lax.rsqrt(jnp.mean(tok * tok, axis=1, keepdims=True) + EPS)
    types = type_ref[...]
    gain_rows = jnp.zeros_like(tok)
    for k in range(TYPES):
        gain_rows = jnp.where(types == k, gain_ref[k : k + 1, :], gain_rows)
    rows = tok.shape[0]
    lanes = lax.broadcasted_iota(jnp.int32, (rows, 128), 1)
    onehot = jnp.where(lanes == types, 1.0, 0.0)
    below = lax.broadcasted_iota(jnp.int32, (rows, rows), 1)
    above = lax.broadcasted_iota(jnp.int32, (rows, rows), 0)
    earlier = jnp.where(below < above, 1.0, 0.0).astype(BF16)
    running = jnp.dot(earlier, onehot.astype(BF16), preferred_element_type=F32)
    rank = jnp.sum(running * onehot, axis=1, keepdims=True).astype(jnp.int32)
    return tok, inverse, types, gain_rows, rank


def wide_mod(value):
    return jnp.where(value >= TYPES, value - TYPES, value)


def slots(lane):
    in_tail = lane >= 2 * MAIN
    left = jnp.where(lane < MAIN, lane, jnp.where(in_tail & (lane < 2 * MAIN + TAIL), lane - MAIN, -1))
    right = jnp.where(
        (lane >= MAIN) & ~in_tail, lane - MAIN, jnp.where(lane >= 2 * MAIN + TAIL, lane - CAP, -1)
    )
    return left, right


def pack_kernel(plane_ref, tokens_ref, grad_ref, type_ref, gain_ref, *outs):
    tok, inverse, types, gain_rows, rank = token_terms(tokens_ref, type_ref, gain_ref)
    rows, width = tok.shape
    half = width // 2
    normed = (tok * inverse * gain_rows).astype(BF16)
    grad = grad_ref[...]
    both_n = jnp.concatenate([normed[:, :half], normed[:, half:]], axis=0)
    both_g = jnp.concatenate([grad[:, :half], grad[:, half:]], axis=0)
    slot_l, slot_r = slots(lax.broadcasted_iota(jnp.int32, (rows, HALF), 1))
    for shift, out in enumerate(outs):
        here = types == wide_mod(plane_ref[0] + shift)
        pick_l = jnp.where(here & (rank == slot_l), 1.0, 0.0)
        pick_r = jnp.where(here & (rank == slot_r), 1.0, 0.0)
        pick = jnp.concatenate([pick_l, pick_r], axis=0).astype(BF16)
        out_n = lax.dot_general(pick, both_n, TN, preferred_element_type=F32)
        out_g = lax.dot_general(pick, both_g, TN, preferred_element_type=F32)
        out[...] = jnp.concatenate(
            [out_n[: 2 * MAIN], out_g[: 2 * MAIN], out_n[2 * MAIN :], out_g[2 * MAIN :]], axis=0
        ).astype(BF16)


def finish_kernel(plane_ref, tokens_ref, grad_ref, type_ref, gain_ref, *refs):
    returned = refs[:TYPES]
    gains = refs[TYPES : 2 * TYPES]
    out, gain_out = refs[2 * TYPES :]
    tok, inverse, types, gain_rows, rank = token_terms(tokens_ref, type_ref, gain_ref)
    rows, width = tok.shape
    slot_l, slot_r = slots(lax.broadcasted_iota(jnp.int32, (rows, HALF), 1))
    left = jnp.zeros((rows, width // 2), F32)
    right = jnp.zeros((rows, width // 2), F32)
    for shift in range(TYPES):
        here = types == wide_mod(plane_ref[0] + shift)
        block = returned[shift][...]
        pick_l = jnp.where(here & (rank == slot_l), 1.0, 0.0).astype(BF16)
        pick_r = jnp.where(here & (rank == slot_r), 1.0, 0.0).astype(BF16)
        left += jnp.dot(pick_l, block, preferred_element_type=F32)
        right += jnp.dot(pick_r, block, preferred_element_type=F32)
    scaled = jnp.concatenate([left, right], axis=1) * gain_rows
    inner = jnp.sum(scaled * tok, axis=1, keepdims=True)
    branch = scaled * inverse - tok * (inner * inverse * inverse * inverse / width)
    out[...] = (grad_ref[...].astype(F32) + branch).astype(BF16)
    row = lax.broadcasted_iota(jnp.int32, (TYPES, width), 0)
    total = jnp.zeros((TYPES, width), F32)
    for shift in range(TYPES):
        kind = wide_mod(plane_ref[0] + TYPES - shift)
        total = jnp.where(row == kind, gains[shift][...], total)
    gain_out[...] = total / gain_ref[...]


def pass_kernel(*refs):
    pass


def gated(value, after):
    return pl.pallas_call(
        pass_kernel,
        in_specs=[HBM] * (1 + len(after)),
        out_specs=HBM,
        out_shape=jax.ShapeDtypeStruct(value.shape, value.dtype),
        input_output_aliases={0: 0},
        compiler_params=params(),
    )(value, *after)


def warm_kernel(up, down, after, out):
    out[...] = jnp.zeros_like(out)


def warmed(up, down, after):
    return pl.pallas_call(
        warm_kernel,
        in_specs=[VMEM] * 2 + [HBM],
        out_specs=VMEM,
        out_shape=jax.ShapeDtypeStruct((8, 128), F32),
        compiler_params=params(),
        cost_estimate=cost(8e9, 8),
    )(up, down, after)


def assemble(blk, normed, grads):
    count, half = blk.shape[0], blk.shape[2]
    low = lax.broadcasted_iota(jnp.int32, (8, half), 0) < TAIL
    for i in range(count):
        into = slice(i * MAIN, (i + 1) * MAIN)
        normed[into, :half] = blk[i, 0:MAIN, :]
        normed[into, half:] = blk[i, MAIN : 2 * MAIN, :]
        grads[into, :half] = blk[i, 2 * MAIN : 3 * MAIN, :]
        grads[into, half:] = blk[i, 3 * MAIN : 4 * MAIN, :]
    tails_n, tails_g = [], []
    for i in range(0, count, 2):
        a = blk[i, 4 * MAIN :, :].astype(F32)
        b = blk[i + 1, 4 * MAIN :, :].astype(F32)
        for first, tails in ((0, tails_n), (8, tails_g)):
            u, v = a[first : first + 8], b[first : first + 8]
            left = jnp.where(low, u, pltpu.roll(v, TAIL, 0))
            right = jnp.where(low, pltpu.roll(u, TAIL, 0), v)
            tails.append(jnp.concatenate([left, right], axis=1))
    normed[count * MAIN :, :] = jnp.concatenate(tails_n, axis=0).astype(BF16)
    grads[count * MAIN :, :] = jnp.concatenate(tails_g, axis=0).astype(BF16)


def forward_kernel(blocks, tile, afters, *refs):
    ins = refs[:blocks]
    up, down = refs[blocks : blocks + 2]
    normed, grads, act, pre, blk, n_v, g_v, act_v, pre_v, in_sem, o_sem = refs[blocks + 2 + afters :]
    hidden = up.shape[1]
    in_copies = [pltpu.make_async_copy(ins[i], blk.at[i], in_sem.at[i]) for i in range(blocks)]
    for copy in in_copies:
        copy.start()
    for copy in in_copies:
        copy.wait()
    assemble(blk, n_v, g_v)
    n_copy = pltpu.make_async_copy(n_v, normed, o_sem.at[0])
    g_copy = pltpu.make_async_copy(g_v, grads, o_sem.at[1])
    for t in range(hidden // tile):
        cols = slice(t * tile, (t + 1) * tile)
        preact = jnp.dot(n_v[...], up[:, cols], preferred_element_type=F32)
        grad_act = lax.dot_general(g_v[...], down[cols, :], NT, preferred_element_type=F32)
        sig = jax.nn.sigmoid(preact)
        act_v[:, cols] = (preact * sig).astype(BF16)
        pre_v[:, cols] = (grad_act * (sig * (1.0 + preact * (1.0 - sig)))).astype(BF16)
        if t == 0:
            n_copy.start()
            g_copy.start()
    last = [
        pltpu.make_async_copy(pre_v, pre, o_sem.at[2]),
        pltpu.make_async_copy(act_v, act, o_sem.at[3]),
    ]
    for copy in last:
        copy.start()
    for copy in [n_copy, g_copy] + last:
        copy.wait()


def forward(blocks, up, down, after):
    width, hidden = up.shape
    rows = len(blocks) * CAP
    tile = FORWARD_TILE if hidden % FORWARD_TILE == 0 else hidden // 2
    shapes = [(rows, width), (rows, width), (rows, hidden), (rows, hidden)]
    return pl.pallas_call(
        functools.partial(forward_kernel, len(blocks), tile, len(after)),
        in_specs=[HBM] * len(blocks) + [VMEM] * 2 + [HBM] * len(after),
        out_specs=[HBM] * len(shapes),
        out_shape=[jax.ShapeDtypeStruct(s, BF16) for s in shapes],
        scratch_shapes=[
            pltpu.VMEM((len(blocks), PAIR, width // 2), BF16),
        ]
        + [pltpu.VMEM(s, BF16) for s in shapes]
        + [
            pltpu.SemaphoreType.DMA((len(blocks),)),
            pltpu.SemaphoreType.DMA((4,)),
        ],
        compiler_params=params(rows),
        cost_estimate=cost(4 * rows * width * hidden, 2 * width * hidden),
    )(*blocks, up, down, *after)


def backward_kernel(shifts, pairs, tile, afters, pre, up, normed, *refs):
    refs = refs[afters:]
    keeps, sends, gain = refs[:pairs], refs[pairs : 2 * pairs], refs[2 * pairs]
    pre_v, n_v, out_v, gain_v, tail_v, in_sem, o_sem = refs[2 * pairs + 1 :]
    width = up.shape[0]
    half = width // 2
    blocks = 2 * shifts * pairs
    sides = blocks // 2
    low = lax.broadcasted_iota(jnp.int32, (8, half), 0) < TAIL
    pre_copy = pltpu.make_async_copy(pre, pre_v, in_sem.at[0])
    pre_copy.start()
    n_copy = pltpu.make_async_copy(normed, n_v, in_sem.at[1])
    n_copy.start()
    pre_copy.wait()
    for t in range(width // tile):
        first = t * tile
        cols = slice(first, first + tile)
        dx = lax.dot_general(pre_v[...], up[cols, :], NT, preferred_element_type=F32)
        if t == 0:
            n_copy.wait()
        gain_v[:, cols] = jnp.sum(dx * n_v[:, cols].astype(F32), axis=0, keepdims=True)
        tail_v[:, cols] = dx[blocks * MAIN :]
        row = MAIN if first >= half else 0
        into = slice(first % half, first % half + tile)
        for number in range(blocks):
            side, at = number // sides, number % sides
            base = at // pairs * 2 * MAIN + row
            block = dx[number * MAIN : (number + 1) * MAIN].astype(BF16)
            out_v[side * pairs + at % pairs, base : base + MAIN, into] = block
    last = []
    for side in (1, 0):
        for j in reversed(range(pairs)):
            tails = []
            for shift in range(shifts):
                number = side * sides + shift * pairs + j
                tail = tail_v[number // 2 * 8 : number // 2 * 8 + 8, :]
                if number % 2 == 0:
                    joined = jnp.where(low, tail[:, :half], pltpu.roll(tail[:, half:], TAIL, 0))
                else:
                    joined = jnp.where(low, pltpu.roll(tail[:, :half], TAIL, 0), tail[:, half:])
                tails.append(joined)
            block = side * pairs + j
            out_v[block, shifts * 2 * MAIN :, :] = jnp.concatenate(tails, axis=0).astype(BF16)
            to = (sends if side else keeps)[j]
            last.append(pltpu.make_async_copy(out_v.at[block], to, o_sem.at[block]))
            last[-1].start()
    last.append(pltpu.make_async_copy(gain_v, gain, o_sem.at[2 * pairs]))
    last[-1].start()
    for copy in last:
        copy.wait()


def backward(pre, up, normed, shifts, pairs, after):
    width, hidden = up.shape
    rows = pre.shape[0]
    tile = min(512, width // 2)
    shape = (shifts * HALF, width // 2)
    outs = [jax.ShapeDtypeStruct(shape, BF16)] * (2 * pairs) + [jax.ShapeDtypeStruct((1, width), F32)]
    result = pl.pallas_call(
        functools.partial(backward_kernel, shifts, pairs, tile, len(after)),
        in_specs=[HBM, VMEM, HBM] + [HBM] * len(after),
        out_specs=[HBM] * len(outs),
        out_shape=outs,
        scratch_shapes=[
            pltpu.VMEM(pre.shape, BF16),
            pltpu.VMEM(normed.shape, BF16),
            pltpu.VMEM((2 * pairs,) + shape, BF16),
            pltpu.VMEM((1, width), F32),
            pltpu.VMEM((2 * shifts * pairs * TAIL, width), F32),
            pltpu.SemaphoreType.DMA((2,)),
            pltpu.SemaphoreType.DMA((len(outs),)),
        ],
        compiler_params=params(rows),
        cost_estimate=cost(2 * rows * width * hidden, 2 * width * hidden),
    )(pre, up, normed, *after)
    return result[:pairs], result[pairs : 2 * pairs], result[2 * pairs]


def merge_kernel(first_ref, second_ref, *refs):
    refs[-1][...] = (first_ref[...].astype(F32) + second_ref[...].astype(F32)).astype(BF16)


def merged(keep, got, after):
    return pl.pallas_call(
        merge_kernel,
        in_specs=[VMEM, VMEM] + [HBM] * len(after),
        out_specs=VMEM,
        out_shape=jax.ShapeDtypeStruct(keep.shape, BF16),
        compiler_params=params(),
    )(keep, got, *after)


def total_kernel(shifts, parts, *refs):
    outs = refs[-shifts:]
    total = refs[0][...].astype(F32)
    for part in refs[1:parts]:
        total = total + part[...].astype(F32)
    mains = shifts * 2 * MAIN
    for s, out in enumerate(outs):
        out[: 2 * MAIN] = total[s * 2 * MAIN : (s + 1) * 2 * MAIN].astype(BF16)
        out[2 * MAIN :] = total[mains + s * 2 * TAIL : mains + (s + 1) * 2 * TAIL].astype(BF16)


def totals(parts, shifts, after):
    return pl.pallas_call(
        functools.partial(total_kernel, shifts, len(parts)),
        in_specs=[VMEM] * len(parts) + [HBM] * len(after),
        out_specs=[VMEM] * shifts,
        out_shape=[jax.ShapeDtypeStruct((HALF, parts[0].shape[1]), BF16)] * shifts,
        compiler_params=params(),
    )(*parts, *after)


def weight_kernel(count, tile, *refs):
    lefts, rights, out, done = refs[:count], refs[count : 2 * count], refs[-3], refs[-2]
    stacked = refs[-1]

    @pl.when(pl.program_id(0) == 0)
    def _():
        first = 0
        for right in rights:
            stacked[first : first + right.shape[0], :] = right[...]
            first += right.shape[0]

    left = jnp.concatenate([ref[...] for ref in lefts], axis=0)
    out[...] = lax.dot_general(left, stacked[...], TN, preferred_element_type=F32).astype(BF16)
    done[...] = jnp.zeros_like(done)


def weight_grad(lefts, rights, after, first=0, count=None, into=None):
    rows = sum(x.shape[0] for x in lefts)
    long, wide = lefts[0].shape[1], rights[0].shape[1]
    tile = min(512, long // 2)
    count = long // tile if count is None else count
    given = [] if into is None else [into]
    operands = [*lefts, *rights, *given, *after]
    return pl.pallas_call(
        functools.partial(weight_kernel, len(lefts), tile),
        grid=(count,),
        in_specs=[pl.BlockSpec((x.shape[0], tile), lambda j: (0, j + first)) for x in lefts]
        + [pl.BlockSpec(x.shape, lambda j: (0, 0)) for x in rights]
        + [HBM] * (len(given) + len(after)),
        out_specs=[pl.BlockSpec((tile, wide), lambda j: (j + first, 0)), pl.BlockSpec((8, 128), lambda j: (0, 0))],
        out_shape=[jax.ShapeDtypeStruct((long, wide), BF16), jax.ShapeDtypeStruct((8, 128), F32)],
        scratch_shapes=[pltpu.VMEM((rows, wide), BF16)],
        input_output_aliases={2 * len(lefts): 0} if given else {},
        compiler_params=params(rows // 2),
        cost_estimate=cost(2 * rows * tile * count * wide, 2 * tile * count * wide),
    )(*operands)


def local(tokens, grad_out, event_type, type_gain, up_weight, down_weight):
    seq = lax.axis_size("seq")
    owners = seq // TYPES
    pairs = owners // CORES
    width = tokens.shape[1]
    plane = (lax.axis_index("seq") // owners).astype(jnp.int32).reshape(1)

    def moved(x, to):
        return lax.ppermute(x, "seq", [(i, to(i)) for i in range(seq)])

    def to_plane(x, shift):
        return moved(x, lambda i: (i + shift * owners) % seq)

    def to_pair(x, shift):
        return moved(x, lambda i: i // owners * owners + (i % owners + CORES * shift) % owners)

    def to_core(x):
        return moved(x, lambda i: i ^ 1)

    packed = pl.pallas_call(
        pack_kernel,
        in_specs=[SMEM] + [VMEM] * 4,
        out_shape=[jax.ShapeDtypeStruct((PAIR, width // 2), BF16)] * TYPES,
        compiler_params=params(2 * tokens.shape[0]),
    )(plane, tokens, grad_out, event_type, type_gain)
    acts, pres, norms, grads, gain_parts, returned = [], [], [], [], [], {}

    def work(rows, cross, after):
        normed, grad, act, pre = forward(rows + cross, up_weight, down_weight, after)
        acts.append(act)
        pres.append(pre)
        norms.append(normed)
        grads.append(grad)
        return pre, normed

    def leave(pre, normed, shifts, after):
        keep, send, gain = backward(pre, up_weight, normed, shifts, pairs, after)
        gain_parts.append(gain)
        return keep, [to_core(x) for x in send[::-1]][::-1]

    def over_cores(kept, after):
        keep, got = kept
        sent = [merged(keep[j], got[j], after) for j in range(1, pairs)]
        return [keep[0], got[0]] + [to_pair(sent[j - 1], pairs - j) for j in range(1, pairs)], sent

    def over_planes(shifts, parts, after):
        sums = totals(parts, len(shifts), after)
        for shift, total in zip(shifts, sums):
            returned[shift] = to_plane(total, TYPES - shift) if shift else total
        return list(sums)[:1]

    def spread(x, after):
        row = [x] + [gated(to_pair(x, j), after) for j in range(1, pairs)]
        return row, [to_core(y) for y in row]

    one, two = to_plane(packed[1], 1), to_plane(packed[2], 2)
    warm = warmed(up_weight, down_weight, packed[0])
    row0, cross0 = spread(packed[0], [warm])
    row1, cross1 = spread(one, [warm])
    two = gated(two, [warm])
    last = gated(packed[3], [two])
    three = to_plane(last, 3)
    pre1, normed1 = work(row0 + row1, cross0 + cross1, [last])
    row2, cross2 = spread(two, [pre1])
    three = gated(three, [pre1])
    kept1 = leave(pre1, normed1, 2, row2[1:] + [three])
    pre2, normed2 = work(row2, cross2, [gain_parts[0]])
    row3, cross3 = spread(three, [pre2])
    parts1, sent1 = over_cores(kept1, [pre2])
    kept2 = leave(pre2, normed2, 1, row3[1:] + sent1)
    pre3, normed3 = work(row3, cross3, [gain_parts[1]])
    parts2, sent2 = over_cores(kept2, [pre3])
    total1 = over_planes((0, 1), parts1, [pre3])
    kept3 = leave(pre3, normed3, 1, sent2 + total1)
    total2 = over_planes((2,), parts2, [gain_parts[2]])
    gain = summed(gain_parts, total2)
    gain = [gain, to_core(gain)]
    tiles = max(2, width // 512)
    split = TILES_FIRST
    grad_up, done = weight_grad(norms, pres, total2 + [gain[0], returned[1]], 0, split)
    parts3, sent3 = over_cores(kept3, [done])
    gain = summed(gain, [done])
    gain = [gain] + [to_pair(gain, j) for j in range(1, pairs)]
    grad_up, done = weight_grad(norms, pres, sent3 + [gain[0]], split, tiles - split, grad_up)
    total3 = over_planes((3,), parts3, [done])
    gain = summed(gain, total3)
    gains = [gain] + [to_plane(gain, shift) for shift in range(1, TYPES)]
    grad_down, done = weight_grad(acts, grads, [gain, returned[2]])
    grad_tokens, grad_gain = pl.pallas_call(
        finish_kernel,
        in_specs=[SMEM] + [VMEM] * (4 + 2 * TYPES),
        out_shape=[
            jax.ShapeDtypeStruct(tokens.shape, BF16),
            jax.ShapeDtypeStruct((TYPES, width), F32),
        ],
        compiler_params=params(2 * tokens.shape[0]),
    )(plane, tokens, grad_out, event_type, type_gain, *[returned[shift] for shift in range(TYPES)], *gains)
    return (grad_tokens, grad_gain, grad_up, grad_down)


def solution(mesh):
    placed = (
        P(("groups", "seq"), None),
        P(("groups", "seq"), None),
        P(("groups", "seq"), None),
        P(),
        P(None, "seq"),
        P("seq", None),
    )
    return jax.shard_map(
        local,
        mesh=mesh,
        in_specs=placed,
        out_specs=(
            P(("groups", "seq"), None),
            P("groups", None),
            P("groups", "seq"),
            P(("groups", "seq"), None),
        ),
        check_vma=False,
    )
```

```python
import functools

import jax
import jax.numpy as jnp
from jax import lax
from jax.experimental import pallas as pl
from jax.experimental.pallas import tpu as pltpu
from jax.sharding import PartitionSpec as P

TYPES = 4
CAP = 36
MAIN = 32
TAIL = CAP - MAIN
HALF = 2 * CAP
PAIR = 2 * HALF
EPS = 1e-06
CORES = 2

F32 = jnp.float32
BF16 = jnp.bfloat16
VMEM_LIMIT = 8 << 20
FORWARD_TILE = 512
HASTE = 100000
TILES_FIRST = 2
NT = (((1,), (1,)), ((), ()))
TN = (((0,), (0,)), ((), ()))
HBM = pl.BlockSpec(memory_space=pltpu.HBM)
VMEM = pl.BlockSpec(memory_space=pltpu.VMEM)
SMEM = pl.BlockSpec(memory_space=pltpu.SMEM)


def params(rows=0, each=40, base=VMEM_LIMIT):
    return pltpu.CompilerParams(vmem_limit_bytes=base + rows * each * 1024)


def cost(flops, moved, haste=HASTE):
    return pl.CostEstimate(flops=int(flops) // haste, bytes_accessed=int(moved) // haste, transcendentals=0)


def sum_kernel(count, *refs):
    refs[-1][...] = sum(ref[...] for ref in refs[:count])


def summed(parts, after):
    return pl.pallas_call(
        functools.partial(sum_kernel, len(parts)),
        in_specs=[VMEM] * len(parts) + [HBM] * len(after),
        out_specs=VMEM,
        out_shape=jax.ShapeDtypeStruct(parts[0].shape, F32),
        compiler_params=params(),
    )(*parts, *after)


def token_terms(tokens_ref, type_ref, gain_ref):
    tok = tokens_ref[...].astype(F32)
    inverse = lax.rsqrt(jnp.mean(tok * tok, axis=1, keepdims=True) + EPS)
    rows = tok.shape[0]
    below = lax.broadcasted_iota(jnp.int32, (rows, rows), 1)
    above = lax.broadcasted_iota(jnp.int32, (rows, rows), 0)
    types = jnp.sum(jnp.where(below == above, type_ref[...], 0), axis=1, keepdims=True)
    gain_rows = jnp.zeros_like(tok)
    for k in range(TYPES):
        gain_rows = jnp.where(types == k, gain_ref[k : k + 1, :], gain_rows)
    lanes = lax.broadcasted_iota(jnp.int32, (rows, 128), 1)
    onehot = jnp.where(lanes == types, 1.0, 0.0)
    earlier = jnp.where(below < above, 1.0, 0.0).astype(BF16)
    running = jnp.dot(earlier, onehot.astype(BF16), preferred_element_type=F32)
    rank = jnp.sum(running * onehot, axis=1, keepdims=True).astype(jnp.int32)
    return tok, inverse, types, gain_rows, rank


def wide_mod(value):
    return jnp.where(value >= TYPES, value - TYPES, value)


def slots(lane):
    in_tail = lane >= 2 * MAIN
    left = jnp.where(lane < MAIN, lane, jnp.where(in_tail & (lane < 2 * MAIN + TAIL), lane - MAIN, -1))
    right = jnp.where(
        (lane >= MAIN) & ~in_tail, lane - MAIN, jnp.where(lane >= 2 * MAIN + TAIL, lane - CAP, -1)
    )
    return left, right


def pack_kernel(plane_ref, tokens_in, grad_in, type_ref, gain_in, *refs):
    outs, (tokens_ref, grad_ref, gain_ref, sem) = refs[:TYPES], refs[TYPES:]
    copies = []
    for i, (source, target) in enumerate(((tokens_in, tokens_ref), (gain_in, gain_ref), (grad_in, grad_ref))):
        copies.append(pltpu.make_async_copy(source, target, sem.at[i]))
        copies[-1].start()
    for copy in copies:
        copy.wait()
    tok, inverse, types, gain_rows, rank = token_terms(tokens_ref, type_ref, gain_ref)
    rows, width = tok.shape
    half = width // 2
    normed = (tok * inverse * gain_rows).astype(BF16)
    grad = grad_ref[...]
    both_n = jnp.concatenate([normed[:, :half], normed[:, half:]], axis=0)
    both_g = jnp.concatenate([grad[:, :half], grad[:, half:]], axis=0)
    slot_l, slot_r = slots(lax.broadcasted_iota(jnp.int32, (rows, HALF), 1))
    for shift, out in enumerate(outs):
        here = types == wide_mod(plane_ref[0] + shift)
        pick_l = jnp.where(here & (rank == slot_l), 1.0, 0.0)
        pick_r = jnp.where(here & (rank == slot_r), 1.0, 0.0)
        pick = jnp.concatenate([pick_l, pick_r], axis=0).astype(BF16)
        out_n = lax.dot_general(pick, both_n, TN, preferred_element_type=F32)
        out_g = lax.dot_general(pick, both_g, TN, preferred_element_type=F32)
        out[...] = jnp.concatenate(
            [out_n[: 2 * MAIN], out_g[: 2 * MAIN], out_n[2 * MAIN :], out_g[2 * MAIN :]], axis=0
        ).astype(BF16)


def finish_kernel(plane_ref, tokens_ref, grad_ref, type_ref, gain_ref, *refs):
    returned = refs[:TYPES]
    gains = refs[TYPES : 2 * TYPES]
    out, gain_out = refs[2 * TYPES :]
    tok, inverse, types, gain_rows, rank = token_terms(tokens_ref, type_ref, gain_ref)
    rows, width = tok.shape
    slot_l, slot_r = slots(lax.broadcasted_iota(jnp.int32, (rows, HALF), 1))
    left = jnp.zeros((rows, width // 2), F32)
    right = jnp.zeros((rows, width // 2), F32)
    for shift in range(TYPES):
        here = types == wide_mod(plane_ref[0] + shift)
        block = returned[shift][...]
        pick_l = jnp.where(here & (rank == slot_l), 1.0, 0.0).astype(BF16)
        pick_r = jnp.where(here & (rank == slot_r), 1.0, 0.0).astype(BF16)
        left += jnp.dot(pick_l, block, preferred_element_type=F32)
        right += jnp.dot(pick_r, block, preferred_element_type=F32)
    scaled = jnp.concatenate([left, right], axis=1) * gain_rows
    inner = jnp.sum(scaled * tok, axis=1, keepdims=True)
    branch = scaled * inverse - tok * (inner * inverse * inverse * inverse / width)
    out[...] = (grad_ref[...].astype(F32) + branch).astype(BF16)
    row = lax.broadcasted_iota(jnp.int32, (TYPES, width), 0)
    total = jnp.zeros((TYPES, width), F32)
    for shift in range(TYPES):
        kind = wide_mod(plane_ref[0] + TYPES - shift)
        total = jnp.where(row == kind, gains[shift][...], total)
    gain_out[...] = total / gain_ref[...]


def pass_kernel(*refs):
    pass


def gated(value, after):
    return pl.pallas_call(
        pass_kernel,
        in_specs=[HBM] * (1 + len(after)),
        out_specs=HBM,
        out_shape=jax.ShapeDtypeStruct(value.shape, value.dtype),
        input_output_aliases={0: 0},
        compiler_params=params(),
    )(value, *after)


def warm_kernel(up, down, after, out):
    out[...] = jnp.zeros_like(out)


def warmed(up, down, after):
    return pl.pallas_call(
        warm_kernel,
        in_specs=[VMEM] * 2 + [HBM],
        out_specs=VMEM,
        out_shape=jax.ShapeDtypeStruct((8, 128), F32),
        compiler_params=params(),
        cost_estimate=cost(8e9, 8, 1),
    )(up, down, after)


def assemble(blk, normed, grads):
    count, half = blk.shape[0], blk.shape[2]
    low = lax.broadcasted_iota(jnp.int32, (8, half), 0) < TAIL
    for i in range(count):
        into = slice(i * MAIN, (i + 1) * MAIN)
        normed[into, :half] = blk[i, 0:MAIN, :]
        normed[into, half:] = blk[i, MAIN : 2 * MAIN, :]
        grads[into, :half] = blk[i, 2 * MAIN : 3 * MAIN, :]
        grads[into, half:] = blk[i, 3 * MAIN : 4 * MAIN, :]
    tails_n, tails_g = [], []
    for i in range(0, count, 2):
        a = blk[i, 4 * MAIN :, :].astype(F32)
        b = blk[i + 1, 4 * MAIN :, :].astype(F32)
        for first, tails in ((0, tails_n), (8, tails_g)):
            u, v = a[first : first + 8], b[first : first + 8]
            left = jnp.where(low, u, pltpu.roll(v, TAIL, 0))
            right = jnp.where(low, pltpu.roll(u, TAIL, 0), v)
            tails.append(jnp.concatenate([left, right], axis=1))
    normed[count * MAIN :, :] = jnp.concatenate(tails_n, axis=0).astype(BF16)
    grads[count * MAIN :, :] = jnp.concatenate(tails_g, axis=0).astype(BF16)


def forward_kernel(blocks, tile, afters, *refs):
    ins = refs[:blocks]
    up, down = refs[blocks : blocks + 2]
    normed, grads, act, pre, blk, n_v, g_v, act_v, pre_v, in_sem, o_sem = refs[blocks + 2 + afters :]
    hidden = up.shape[1]
    in_copies = [pltpu.make_async_copy(ins[i], blk.at[i], in_sem.at[i]) for i in range(blocks)]
    for copy in in_copies:
        copy.start()
    for copy in in_copies:
        copy.wait()
    assemble(blk, n_v, g_v)
    n_copy = pltpu.make_async_copy(n_v, normed, o_sem.at[0])
    g_copy = pltpu.make_async_copy(g_v, grads, o_sem.at[1])
    for t in range(hidden // tile):
        cols = slice(t * tile, (t + 1) * tile)
        preact = jnp.dot(n_v[...], up[:, cols], preferred_element_type=F32)
        grad_act = lax.dot_general(g_v[...], down[cols, :], NT, preferred_element_type=F32)
        sig = jax.nn.sigmoid(preact)
        act_v[:, cols] = (preact * sig).astype(BF16)
        pre_v[:, cols] = (grad_act * (sig * (1.0 + preact * (1.0 - sig)))).astype(BF16)
        if t == 0:
            n_copy.start()
            g_copy.start()
    last = [
        pltpu.make_async_copy(pre_v, pre, o_sem.at[2]),
        pltpu.make_async_copy(act_v, act, o_sem.at[3]),
    ]
    for copy in last:
        copy.start()
    for copy in [n_copy, g_copy] + last:
        copy.wait()


def forward(blocks, up, down, after):
    width, hidden = up.shape
    rows = len(blocks) * CAP
    tile = FORWARD_TILE if hidden % FORWARD_TILE == 0 else hidden // 2
    shapes = [(rows, width), (rows, width), (rows, hidden), (rows, hidden)]
    return pl.pallas_call(
        functools.partial(forward_kernel, len(blocks), tile, len(after)),
        in_specs=[HBM] * len(blocks) + [VMEM] * 2 + [HBM] * len(after),
        out_specs=[HBM] * len(shapes),
        out_shape=[jax.ShapeDtypeStruct(s, BF16) for s in shapes],
        scratch_shapes=[
            pltpu.VMEM((len(blocks), PAIR, width // 2), BF16),
        ]
        + [pltpu.VMEM(s, BF16) for s in shapes]
        + [
            pltpu.SemaphoreType.DMA((len(blocks),)),
            pltpu.SemaphoreType.DMA((4,)),
        ],
        compiler_params=params(rows, 26, 5 << 20),
        cost_estimate=cost(4 * rows * width * hidden, 2 * width * hidden),
    )(*blocks, up, down, *after)


def backward_kernel(shifts, pairs, tile, afters, pre, up, normed, *refs):
    refs = refs[afters:]
    keeps, sends, gain = refs[:pairs], refs[pairs : 2 * pairs], refs[2 * pairs]
    pre_v, n_v, out_v, gain_v, tail_v, in_sem, o_sem = refs[2 * pairs + 1 :]
    width = up.shape[0]
    half = width // 2
    blocks = 2 * shifts * pairs
    sides = blocks // 2
    low = lax.broadcasted_iota(jnp.int32, (8, half), 0) < TAIL
    pre_copy = pltpu.make_async_copy(pre, pre_v, in_sem.at[0])
    pre_copy.start()
    n_copy = pltpu.make_async_copy(normed, n_v, in_sem.at[1])
    n_copy.start()
    pre_copy.wait()
    for t in range(width // tile):
        first = t * tile
        cols = slice(first, first + tile)
        dx = lax.dot_general(pre_v[...], up[cols, :], NT, preferred_element_type=F32)
        if t == 0:
            n_copy.wait()
        gain_v[:, cols] = jnp.sum(dx * n_v[:, cols].astype(F32), axis=0, keepdims=True)
        tail_v[:, cols] = dx[blocks * MAIN :]
        row = MAIN if first >= half else 0
        into = slice(first % half, first % half + tile)
        for number in range(blocks):
            side, at = number // sides, number % sides
            base = at // pairs * 2 * MAIN + row
            block = dx[number * MAIN : (number + 1) * MAIN].astype(BF16)
            out_v[side * pairs + at % pairs, base : base + MAIN, into] = block
    last = []
    for side in (1, 0):
        for j in reversed(range(pairs)):
            tails = []
            for shift in range(shifts):
                number = side * sides + shift * pairs + j
                tail = tail_v[number // 2 * 8 : number // 2 * 8 + 8, :]
                if number % 2 == 0:
                    joined = jnp.where(low, tail[:, :half], pltpu.roll(tail[:, half:], TAIL, 0))
                else:
                    joined = jnp.where(low, pltpu.roll(tail[:, :half], TAIL, 0), tail[:, half:])
                tails.append(joined)
            block = side * pairs + j
            out_v[block, shifts * 2 * MAIN :, :] = jnp.concatenate(tails, axis=0).astype(BF16)
            to = (sends if side else keeps)[j]
            last.append(pltpu.make_async_copy(out_v.at[block], to, o_sem.at[block]))
            last[-1].start()
    last.append(pltpu.make_async_copy(gain_v, gain, o_sem.at[2 * pairs]))
    last[-1].start()
    for copy in last:
        copy.wait()


def backward(pre, up, normed, shifts, pairs, after, haste):
    width, hidden = up.shape
    rows = pre.shape[0]
    tile = min(512, width // 2)
    shape = (shifts * HALF, width // 2)
    outs = [jax.ShapeDtypeStruct(shape, BF16)] * (2 * pairs) + [jax.ShapeDtypeStruct((1, width), F32)]
    result = pl.pallas_call(
        functools.partial(backward_kernel, shifts, pairs, tile, len(after)),
        in_specs=[HBM, VMEM, HBM] + [HBM] * len(after),
        out_specs=[HBM] * len(outs),
        out_shape=outs,
        scratch_shapes=[
            pltpu.VMEM(pre.shape, BF16),
            pltpu.VMEM(normed.shape, BF16),
            pltpu.VMEM((2 * pairs,) + shape, BF16),
            pltpu.VMEM((1, width), F32),
            pltpu.VMEM((2 * shifts * pairs * TAIL, width), F32),
            pltpu.SemaphoreType.DMA((2,)),
            pltpu.SemaphoreType.DMA((len(outs),)),
        ],
        compiler_params=params(rows, 16, 4 << 20),
        cost_estimate=cost(2 * rows * width * hidden, 2 * width * hidden, haste),
    )(pre, up, normed, *after)
    return result[:pairs], result[pairs : 2 * pairs], result[2 * pairs]


def merge_kernel(first_ref, second_ref, *refs):
    refs[-1][...] = (first_ref[...].astype(F32) + second_ref[...].astype(F32)).astype(BF16)


def merged(keep, got, after):
    return pl.pallas_call(
        merge_kernel,
        in_specs=[VMEM, VMEM] + [HBM] * len(after),
        out_specs=VMEM,
        out_shape=jax.ShapeDtypeStruct(keep.shape, BF16),
        compiler_params=params(),
    )(keep, got, *after)


def total_kernel(shifts, parts, *refs):
    outs = refs[-shifts:]
    total = refs[0][...].astype(F32)
    for part in refs[1:parts]:
        total = total + part[...].astype(F32)
    mains = shifts * 2 * MAIN
    for s, out in enumerate(outs):
        out[: 2 * MAIN] = total[s * 2 * MAIN : (s + 1) * 2 * MAIN].astype(BF16)
        out[2 * MAIN :] = total[mains + s * 2 * TAIL : mains + (s + 1) * 2 * TAIL].astype(BF16)


def totals(parts, shifts, after):
    return pl.pallas_call(
        functools.partial(total_kernel, shifts, len(parts)),
        in_specs=[VMEM] * len(parts) + [HBM] * len(after),
        out_specs=[VMEM] * shifts,
        out_shape=[jax.ShapeDtypeStruct((HALF, parts[0].shape[1]), BF16)] * shifts,
        compiler_params=params(),
    )(*parts, *after)


def weight_kernel(count, tile, *refs):
    lefts, rights, out, done = refs[:count], refs[count : 2 * count], refs[-3], refs[-2]
    stacked = refs[-1]

    @pl.when(pl.program_id(0) == 0)
    def _():
        first = 0
        for right in rights:
            stacked[first : first + right.shape[0], :] = right[...]
            first += right.shape[0]

    left = jnp.concatenate([ref[...] for ref in lefts], axis=0)
    out[...] = lax.dot_general(left, stacked[...], TN, preferred_element_type=F32).astype(BF16)
    done[...] = jnp.zeros_like(done)


def weight_grad(lefts, rights, after, first=0, count=None, into=None):
    rows = sum(x.shape[0] for x in lefts)
    long, wide = lefts[0].shape[1], rights[0].shape[1]
    tile = min(512, long // 2)
    count = long // tile if count is None else count
    given = [] if into is None else [into]
    operands = [*lefts, *rights, *given, *after]
    return pl.pallas_call(
        functools.partial(weight_kernel, len(lefts), tile),
        grid=(count,),
        in_specs=[pl.BlockSpec((x.shape[0], tile), lambda j: (0, j + first)) for x in lefts]
        + [pl.BlockSpec(x.shape, lambda j: (0, 0)) for x in rights]
        + [HBM] * (len(given) + len(after)),
        out_specs=[pl.BlockSpec((tile, wide), lambda j: (j + first, 0)), pl.BlockSpec((8, 128), lambda j: (0, 0))],
        out_shape=[jax.ShapeDtypeStruct((long, wide), BF16), jax.ShapeDtypeStruct((8, 128), F32)],
        scratch_shapes=[pltpu.VMEM((rows, wide), BF16)],
        input_output_aliases={2 * len(lefts): 0} if given else {},
        compiler_params=params(rows // 2),
        cost_estimate=cost(2 * rows * tile * count * wide, 2 * tile * count * wide, 1),
    )(*operands)


def local(tokens, grad_out, event_type, type_gain, up_weight, down_weight):
    seq = lax.axis_size("seq")
    owners = seq // TYPES
    pairs = owners // CORES
    width = tokens.shape[1]
    event_type = event_type.reshape(1, -1)
    plane = lax.div(lax.axis_index("seq"), jnp.int32(owners)).reshape(1)

    def moved(x, to):
        return lax.ppermute(x, "seq", [(i, to(i)) for i in range(seq)])

    def to_plane(x, shift):
        return moved(x, lambda i: (i + shift * owners) % seq)

    def to_pair(x, shift):
        return moved(x, lambda i: i // owners * owners + (i % owners + CORES * shift) % owners)

    def to_core(x):
        return moved(x, lambda i: i ^ 1)

    packed = pl.pallas_call(
        pack_kernel,
        in_specs=[SMEM, HBM, HBM, VMEM, HBM],
        out_shape=[jax.ShapeDtypeStruct((PAIR, width // 2), BF16)] * TYPES,
        scratch_shapes=[
            pltpu.VMEM(tokens.shape, BF16),
            pltpu.VMEM(grad_out.shape, BF16),
            pltpu.VMEM(type_gain.shape, F32),
            pltpu.SemaphoreType.DMA((3,)),
        ],
        compiler_params=params(0, 0, 60 << 20),
    )(plane, tokens, grad_out, event_type, type_gain)
    acts, pres, norms, grads, gain_parts, returned = [], [], [], [], [], {}

    def work(rows, cross, after):
        normed, grad, act, pre = forward(rows + cross, up_weight, down_weight, after)
        acts.append(act)
        pres.append(pre)
        norms.append(normed)
        grads.append(grad)
        return pre, normed

    def leave(pre, normed, shifts, after, haste=HASTE):
        keep, send, gain = backward(pre, up_weight, normed, shifts, pairs, after, haste)
        gain_parts.append(gain)
        return keep, [to_core(x) for x in send[::-1]][::-1]

    def over_cores(kept, after):
        keep, got = kept
        sent = [merged(keep[j], got[j], after) for j in range(1, pairs)]
        return [keep[0], got[0]] + [to_pair(sent[j - 1], pairs - j) for j in range(1, pairs)], sent

    def over_planes(shifts, parts, after):
        sums = totals(parts, len(shifts), after)
        for shift, total in zip(shifts, sums):
            returned[shift] = to_plane(total, TYPES - shift) if shift else total
        return list(sums)[:1]

    def spread(x, after):
        row = [x] + [gated(to_pair(x, j), after) for j in range(1, pairs)]
        return row, [to_core(y) for y in row]

    one, two = to_plane(packed[1], 1), to_plane(packed[2], 2)
    warm = warmed(up_weight, down_weight, packed[0])
    row0, cross0 = spread(packed[0], [warm])
    row1, cross1 = spread(one, [warm])
    two = gated(two, [warm])
    last = gated(packed[3], [two])
    three = to_plane(last, 3)
    pre1, normed1 = work(row0 + row1, cross0 + cross1, [last])
    row2, cross2 = spread(two, [pre1])
    three = gated(three, [pre1])
    kept1 = leave(pre1, normed1, 2, row2[1:] + [three], 1)
    pre2, normed2 = work(row2, cross2, [gain_parts[0]])
    row3, cross3 = spread(three, [pre2])
    parts1, sent1 = over_cores(kept1, [pre2])
    kept2 = leave(pre2, normed2, 1, row3[1:] + sent1)
    pre3, normed3 = work(row3, cross3, [gain_parts[1]])
    parts2, sent2 = over_cores(kept2, [pre3])
    kept3 = leave(pre3, normed3, 1, sent2)
    total1 = over_planes((0, 1), parts1, [gain_parts[2]])
    total2 = over_planes((2,), parts2, total1)
    gain = summed(gain_parts, total2)
    gain = summed([gain, to_core(gain)], [])
    gain = summed([gain] + [to_pair(gain, j) for j in range(1, pairs)], [])
    gains = [gain] + [to_plane(gain, shift) for shift in range(1, TYPES)]
    tiles = max(2, width // 512)
    split = TILES_FIRST
    grad_up, done = weight_grad(norms, pres, total2, 0, split)
    parts3, sent3 = over_cores(kept3, [done])
    grad_up, done = weight_grad(norms, pres, sent3 + [returned[1]], split, tiles - split, grad_up)
    total3 = over_planes((3,), parts3, [done])
    grad_down, done = weight_grad(acts, grads, total3 + [returned[2]])
    grad_tokens, grad_gain = pl.pallas_call(
        finish_kernel,
        in_specs=[SMEM] + [VMEM] * (4 + 2 * TYPES),
        out_shape=[
            jax.ShapeDtypeStruct(tokens.shape, BF16),
            jax.ShapeDtypeStruct((TYPES, width), F32),
        ],
        compiler_params=params(2 * tokens.shape[0]),
    )(plane, tokens, grad_out, event_type, type_gain, *[returned[shift] for shift in range(TYPES)], *gains)
    return (grad_tokens, grad_gain, grad_up, grad_down)


def solution(mesh):
    placed = (
        P(("groups", "seq"), None),
        P(("groups", "seq"), None),
        P(("groups", "seq"), None),
        P(),
        P(None, "seq"),
        P("seq", None),
    )
    return jax.shard_map(
        local,
        mesh=mesh,
        in_specs=placed,
        out_specs=(
            P(("groups", "seq"), None),
            P("groups", None),
            P("groups", "seq"),
            P(("groups", "seq"), None),
        ),
        check_vma=False,
    )
```

```python
import functools

import jax
import jax.numpy as jnp
from jax import lax
from jax.experimental import pallas as pl
from jax.experimental.pallas import tpu as pltpu
from jax.sharding import PartitionSpec as P

TYPES = 4
CAP = 36
MAIN = 32
TAIL = CAP - MAIN
HALF = 2 * CAP
PAIR = 2 * HALF
EPS = 1e-06
CORES = 2

F32 = jnp.float32
BF16 = jnp.bfloat16
VMEM_LIMIT = 8 << 20
FORWARD_TILE = 512
HASTE = 100000
TILES_FIRST = 2
NT = (((1,), (1,)), ((), ()))
TN = (((0,), (0,)), ((), ()))
HBM = pl.BlockSpec(memory_space=pltpu.HBM)
VMEM = pl.BlockSpec(memory_space=pltpu.VMEM)
SMEM = pl.BlockSpec(memory_space=pltpu.SMEM)


def params(rows=0, each=40, base=VMEM_LIMIT):
    return pltpu.CompilerParams(vmem_limit_bytes=base + rows * each * 1024)


def cost(flops, moved, haste=HASTE):
    return pl.CostEstimate(flops=int(flops) // haste, bytes_accessed=int(moved) // haste, transcendentals=0)


def sum_kernel(count, *refs):
    refs[-1][...] = sum(ref[...] for ref in refs[:count])


def summed(parts, after):
    return pl.pallas_call(
        functools.partial(sum_kernel, len(parts)),
        in_specs=[VMEM] * len(parts) + [HBM] * len(after),
        out_specs=VMEM,
        out_shape=jax.ShapeDtypeStruct(parts[0].shape, F32),
        compiler_params=params(),
    )(*parts, *after)


def token_terms(tokens_ref, type_ref, gain_ref):
    tok = tokens_ref[...].astype(F32)
    inverse = lax.rsqrt(jnp.mean(tok * tok, axis=1, keepdims=True) + EPS)
    rows = tok.shape[0]
    below = lax.broadcasted_iota(jnp.int32, (rows, rows), 1)
    above = lax.broadcasted_iota(jnp.int32, (rows, rows), 0)
    types = jnp.sum(jnp.where(below == above, type_ref[...], 0), axis=1, keepdims=True)
    gain_rows = jnp.zeros_like(tok)
    for k in range(TYPES):
        gain_rows = jnp.where(types == k, gain_ref[k : k + 1, :], gain_rows)
    lanes = lax.broadcasted_iota(jnp.int32, (rows, 128), 1)
    onehot = jnp.where(lanes == types, 1.0, 0.0)
    earlier = jnp.where(below < above, 1.0, 0.0).astype(BF16)
    running = jnp.dot(earlier, onehot.astype(BF16), preferred_element_type=F32)
    rank = jnp.sum(running * onehot, axis=1, keepdims=True).astype(jnp.int32)
    return tok, inverse, types, gain_rows, rank


def wide_mod(value):
    return jnp.where(value >= TYPES, value - TYPES, value)


def slots(lane):
    in_tail = lane >= 2 * MAIN
    left = jnp.where(lane < MAIN, lane, jnp.where(in_tail & (lane < 2 * MAIN + TAIL), lane - MAIN, -1))
    right = jnp.where(
        (lane >= MAIN) & ~in_tail, lane - MAIN, jnp.where(lane >= 2 * MAIN + TAIL, lane - CAP, -1)
    )
    return left, right


def pack_kernel(plane_ref, tokens_in, grad_in, type_ref, gain_in, *refs):
    outs, (tokens_ref, grad_ref, gain_ref, sem) = refs[:TYPES], refs[TYPES:]
    copies = []
    for i, (source, target) in enumerate(((tokens_in, tokens_ref), (gain_in, gain_ref), (grad_in, grad_ref))):
        copies.append(pltpu.make_async_copy(source, target, sem.at[i]))
        copies[-1].start()
    for copy in copies:
        copy.wait()
    tok, inverse, types, gain_rows, rank = token_terms(tokens_ref, type_ref, gain_ref)
    rows, width = tok.shape
    half = width // 2
    normed = (tok * inverse * gain_rows).astype(BF16)
    grad = grad_ref[...]
    both_n = jnp.concatenate([normed[:, :half], normed[:, half:]], axis=0)
    both_g = jnp.concatenate([grad[:, :half], grad[:, half:]], axis=0)
    slot_l, slot_r = slots(lax.broadcasted_iota(jnp.int32, (rows, HALF), 1))
    for shift, out in enumerate(outs):
        here = types == wide_mod(plane_ref[0] + shift)
        pick_l = jnp.where(here & (rank == slot_l), 1.0, 0.0)
        pick_r = jnp.where(here & (rank == slot_r), 1.0, 0.0)
        pick = jnp.concatenate([pick_l, pick_r], axis=0).astype(BF16)
        out_n = lax.dot_general(pick, both_n, TN, preferred_element_type=F32)
        out_g = lax.dot_general(pick, both_g, TN, preferred_element_type=F32)
        out[...] = jnp.concatenate(
            [out_n[: 2 * MAIN], out_g[: 2 * MAIN], out_n[2 * MAIN :], out_g[2 * MAIN :]], axis=0
        ).astype(BF16)


def finish_kernel(plane_ref, tokens_ref, grad_ref, type_ref, gain_ref, *refs):
    returned = refs[:TYPES]
    gains = refs[TYPES : 2 * TYPES]
    out, gain_out = refs[2 * TYPES :]
    tok, inverse, types, gain_rows, rank = token_terms(tokens_ref, type_ref, gain_ref)
    rows, width = tok.shape
    slot_l, slot_r = slots(lax.broadcasted_iota(jnp.int32, (rows, HALF), 1))
    left = jnp.zeros((rows, width // 2), F32)
    right = jnp.zeros((rows, width // 2), F32)
    for shift in range(TYPES):
        here = types == wide_mod(plane_ref[0] + shift)
        block = returned[shift][...]
        pick_l = jnp.where(here & (rank == slot_l), 1.0, 0.0).astype(BF16)
        pick_r = jnp.where(here & (rank == slot_r), 1.0, 0.0).astype(BF16)
        left += jnp.dot(pick_l, block, preferred_element_type=F32)
        right += jnp.dot(pick_r, block, preferred_element_type=F32)
    scaled = jnp.concatenate([left, right], axis=1) * gain_rows
    inner = jnp.sum(scaled * tok, axis=1, keepdims=True)
    branch = scaled * inverse - tok * (inner * inverse * inverse * inverse / width)
    out[...] = (grad_ref[...].astype(F32) + branch).astype(BF16)
    row = lax.broadcasted_iota(jnp.int32, (TYPES, width), 0)
    total = jnp.zeros((TYPES, width), F32)
    for shift in range(TYPES):
        kind = wide_mod(plane_ref[0] + TYPES - shift)
        total = jnp.where(row == kind, gains[shift][...], total)
    gain_out[...] = total / gain_ref[...]


def pass_kernel(*refs):
    pass


def gated(value, after):
    return pl.pallas_call(
        pass_kernel,
        in_specs=[HBM] * (1 + len(after)),
        out_specs=HBM,
        out_shape=jax.ShapeDtypeStruct(value.shape, value.dtype),
        input_output_aliases={0: 0},
        compiler_params=params(),
    )(value, *after)


def turn_kernel(down, after, out):
    out[...] = down[...].T


def turned(down, after):
    hidden, width = down.shape
    tile = 256
    return pl.pallas_call(
        turn_kernel,
        grid=(hidden // tile,),
        in_specs=[pl.BlockSpec((tile, width), lambda j: (j, 0)), HBM],
        out_specs=pl.BlockSpec((width, tile), lambda j: (0, j)),
        out_shape=jax.ShapeDtypeStruct((width, hidden), BF16),
        compiler_params=params(0, 0, 9 << 20),
        cost_estimate=cost(8e9, 8),
    )(down, after)


def warm_kernel(up, down, after, out):
    out[...] = jnp.zeros_like(out)


def warmed(up, down, after):
    return pl.pallas_call(
        warm_kernel,
        in_specs=[VMEM] * 2 + [HBM],
        out_specs=VMEM,
        out_shape=jax.ShapeDtypeStruct((8, 128), F32),
        compiler_params=params(),
        cost_estimate=cost(8e9, 8, 1),
    )(up, down, after)


def assemble(blk, normed, grads):
    count, half = blk.shape[0], blk.shape[2]
    low = lax.broadcasted_iota(jnp.int32, (8, half), 0) < TAIL
    for i in range(count):
        into = slice(i * MAIN, (i + 1) * MAIN)
        normed[into, :half] = blk[i, 0:MAIN, :]
        normed[into, half:] = blk[i, MAIN : 2 * MAIN, :]
        grads[into, :half] = blk[i, 2 * MAIN : 3 * MAIN, :]
        grads[into, half:] = blk[i, 3 * MAIN : 4 * MAIN, :]
    tails_n, tails_g = [], []
    for i in range(0, count, 2):
        a = blk[i, 4 * MAIN :, :].astype(F32)
        b = blk[i + 1, 4 * MAIN :, :].astype(F32)
        for first, tails in ((0, tails_n), (8, tails_g)):
            u, v = a[first : first + 8], b[first : first + 8]
            left = jnp.where(low, u, pltpu.roll(v, TAIL, 0))
            right = jnp.where(low, pltpu.roll(u, TAIL, 0), v)
            tails.append(jnp.concatenate([left, right], axis=1))
    normed[count * MAIN :, :] = jnp.concatenate(tails_n, axis=0).astype(BF16)
    grads[count * MAIN :, :] = jnp.concatenate(tails_g, axis=0).astype(BF16)


def forward_kernel(blocks, tile, afters, *refs):
    ins = refs[:blocks]
    up, down = refs[blocks : blocks + 2]
    normed, grads, act, pre, blk, n_v, g_v, act_v, pre_v, in_sem, o_sem = refs[blocks + 2 + afters :]
    hidden = up.shape[1]
    in_copies = [pltpu.make_async_copy(ins[i], blk.at[i], in_sem.at[i]) for i in range(blocks)]
    for copy in in_copies:
        copy.start()
    for copy in in_copies:
        copy.wait()
    assemble(blk, n_v, g_v)
    n_copy = pltpu.make_async_copy(n_v, normed, o_sem.at[0])
    g_copy = pltpu.make_async_copy(g_v, grads, o_sem.at[1])
    for t in range(hidden // tile):
        cols = slice(t * tile, (t + 1) * tile)
        preact = jnp.dot(n_v[...], up[:, cols], preferred_element_type=F32)
        grad_act = jnp.dot(g_v[...], down[:, cols], preferred_element_type=F32)
        sig = jax.nn.sigmoid(preact)
        act_v[:, cols] = (preact * sig).astype(BF16)
        pre_v[:, cols] = (grad_act * (sig * (1.0 + preact * (1.0 - sig)))).astype(BF16)
        if t == 0:
            n_copy.start()
            g_copy.start()
    last = [
        pltpu.make_async_copy(pre_v, pre, o_sem.at[2]),
        pltpu.make_async_copy(act_v, act, o_sem.at[3]),
    ]
    for copy in last:
        copy.start()
    for copy in [n_copy, g_copy] + last:
        copy.wait()


def forward(blocks, up, down, after):
    width, hidden = up.shape
    rows = len(blocks) * CAP
    tile = FORWARD_TILE if hidden % FORWARD_TILE == 0 else hidden // 2
    shapes = [(rows, width), (rows, width), (rows, hidden), (rows, hidden)]
    return pl.pallas_call(
        functools.partial(forward_kernel, len(blocks), tile, len(after)),
        in_specs=[HBM] * len(blocks) + [VMEM] * 2 + [HBM] * len(after),
        out_specs=[HBM] * len(shapes),
        out_shape=[jax.ShapeDtypeStruct(s, BF16) for s in shapes],
        scratch_shapes=[
            pltpu.VMEM((len(blocks), PAIR, width // 2), BF16),
        ]
        + [pltpu.VMEM(s, BF16) for s in shapes]
        + [
            pltpu.SemaphoreType.DMA((len(blocks),)),
            pltpu.SemaphoreType.DMA((4,)),
        ],
        compiler_params=params(rows, 26, 5 << 20),
        cost_estimate=cost(4 * rows * width * hidden, 2 * width * hidden),
    )(*blocks, up, down, *after)


def backward_kernel(shifts, pairs, tile, afters, pre, up, normed, *refs):
    refs = refs[afters:]
    keeps, sends, gain = refs[:pairs], refs[pairs : 2 * pairs], refs[2 * pairs]
    pre_v, n_v, out_v, gain_v, tail_v, in_sem, o_sem = refs[2 * pairs + 1 :]
    width = up.shape[0]
    half = width // 2
    blocks = 2 * shifts * pairs
    sides = blocks // 2
    low = lax.broadcasted_iota(jnp.int32, (8, half), 0) < TAIL
    pre_copy = pltpu.make_async_copy(pre, pre_v, in_sem.at[0])
    pre_copy.start()
    n_copy = pltpu.make_async_copy(normed, n_v, in_sem.at[1])
    n_copy.start()
    pre_copy.wait()
    for t in range(width // tile):
        first = t * tile
        cols = slice(first, first + tile)
        dx = lax.dot_general(pre_v[...], up[cols, :], NT, preferred_element_type=F32)
        if t == 0:
            n_copy.wait()
        gain_v[:, cols] = jnp.sum(dx * n_v[:, cols].astype(F32), axis=0, keepdims=True)
        tail_v[:, cols] = dx[blocks * MAIN :]
        row = MAIN if first >= half else 0
        into = slice(first % half, first % half + tile)
        for number in range(blocks):
            side, at = number // sides, number % sides
            base = at // pairs * 2 * MAIN + row
            block = dx[number * MAIN : (number + 1) * MAIN].astype(BF16)
            out_v[side * pairs + at % pairs, base : base + MAIN, into] = block
    last = []
    for side in (1, 0):
        for j in reversed(range(pairs)):
            tails = []
            for shift in range(shifts):
                number = side * sides + shift * pairs + j
                tail = tail_v[number // 2 * 8 : number // 2 * 8 + 8, :]
                if number % 2 == 0:
                    joined = jnp.where(low, tail[:, :half], pltpu.roll(tail[:, half:], TAIL, 0))
                else:
                    joined = jnp.where(low, pltpu.roll(tail[:, :half], TAIL, 0), tail[:, half:])
                tails.append(joined)
            block = side * pairs + j
            out_v[block, shifts * 2 * MAIN :, :] = jnp.concatenate(tails, axis=0).astype(BF16)
            to = (sends if side else keeps)[j]
            last.append(pltpu.make_async_copy(out_v.at[block], to, o_sem.at[block]))
            last[-1].start()
    last.append(pltpu.make_async_copy(gain_v, gain, o_sem.at[2 * pairs]))
    last[-1].start()
    for copy in last:
        copy.wait()


def backward(pre, up, normed, shifts, pairs, after, haste):
    width, hidden = up.shape
    rows = pre.shape[0]
    tile = min(512, width // 2)
    shape = (shifts * HALF, width // 2)
    outs = [jax.ShapeDtypeStruct(shape, BF16)] * (2 * pairs) + [jax.ShapeDtypeStruct((1, width), F32)]
    result = pl.pallas_call(
        functools.partial(backward_kernel, shifts, pairs, tile, len(after)),
        in_specs=[HBM, VMEM, HBM] + [HBM] * len(after),
        out_specs=[HBM] * len(outs),
        out_shape=outs,
        scratch_shapes=[
            pltpu.VMEM(pre.shape, BF16),
            pltpu.VMEM(normed.shape, BF16),
            pltpu.VMEM((2 * pairs,) + shape, BF16),
            pltpu.VMEM((1, width), F32),
            pltpu.VMEM((2 * shifts * pairs * TAIL, width), F32),
            pltpu.SemaphoreType.DMA((2,)),
            pltpu.SemaphoreType.DMA((len(outs),)),
        ],
        compiler_params=params(rows, 16, 4 << 20),
        cost_estimate=cost(2 * rows * width * hidden, 2 * width * hidden, haste),
    )(pre, up, normed, *after)
    return result[:pairs], result[pairs : 2 * pairs], result[2 * pairs]


def merge_kernel(first_ref, second_ref, *refs):
    refs[-1][...] = (first_ref[...].astype(F32) + second_ref[...].astype(F32)).astype(BF16)


def merged(keep, got, after):
    return pl.pallas_call(
        merge_kernel,
        in_specs=[VMEM, VMEM] + [HBM] * len(after),
        out_specs=VMEM,
        out_shape=jax.ShapeDtypeStruct(keep.shape, BF16),
        compiler_params=params(),
    )(keep, got, *after)


def total_kernel(shifts, parts, *refs):
    outs = refs[-shifts:]
    total = refs[0][...].astype(F32)
    for part in refs[1:parts]:
        total = total + part[...].astype(F32)
    mains = shifts * 2 * MAIN
    for s, out in enumerate(outs):
        out[: 2 * MAIN] = total[s * 2 * MAIN : (s + 1) * 2 * MAIN].astype(BF16)
        out[2 * MAIN :] = total[mains + s * 2 * TAIL : mains + (s + 1) * 2 * TAIL].astype(BF16)


def totals(parts, shifts, after):
    return pl.pallas_call(
        functools.partial(total_kernel, shifts, len(parts)),
        in_specs=[VMEM] * len(parts) + [HBM] * len(after),
        out_specs=[VMEM] * shifts,
        out_shape=[jax.ShapeDtypeStruct((HALF, parts[0].shape[1]), BF16)] * shifts,
        compiler_params=params(),
    )(*parts, *after)


def weight_kernel(count, tile, *refs):
    lefts, rights, out, done = refs[:count], refs[count : 2 * count], refs[-3], refs[-2]
    stacked = refs[-1]

    @pl.when(pl.program_id(0) == 0)
    def _():
        first = 0
        for right in rights:
            stacked[first : first + right.shape[0], :] = right[...]
            first += right.shape[0]

    left = jnp.concatenate([ref[...] for ref in lefts], axis=0)
    out[...] = lax.dot_general(left, stacked[...], TN, preferred_element_type=F32).astype(BF16)
    done[...] = jnp.zeros_like(done)


def weight_grad(lefts, rights, after, first=0, count=None, into=None):
    rows = sum(x.shape[0] for x in lefts)
    long, wide = lefts[0].shape[1], rights[0].shape[1]
    tile = min(512, long // 2)
    count = long // tile if count is None else count
    given = [] if into is None else [into]
    operands = [*lefts, *rights, *given, *after]
    return pl.pallas_call(
        functools.partial(weight_kernel, len(lefts), tile),
        grid=(count,),
        in_specs=[pl.BlockSpec((x.shape[0], tile), lambda j: (0, j + first)) for x in lefts]
        + [pl.BlockSpec(x.shape, lambda j: (0, 0)) for x in rights]
        + [HBM] * (len(given) + len(after)),
        out_specs=[pl.BlockSpec((tile, wide), lambda j: (j + first, 0)), pl.BlockSpec((8, 128), lambda j: (0, 0))],
        out_shape=[jax.ShapeDtypeStruct((long, wide), BF16), jax.ShapeDtypeStruct((8, 128), F32)],
        scratch_shapes=[pltpu.VMEM((rows, wide), BF16)],
        input_output_aliases={2 * len(lefts): 0} if given else {},
        compiler_params=params(rows // 2),
        cost_estimate=cost(2 * rows * tile * count * wide, 2 * tile * count * wide, 1),
    )(*operands)


def local(tokens, grad_out, event_type, type_gain, up_weight, down_weight):
    seq = lax.axis_size("seq")
    owners = seq // TYPES
    pairs = owners // CORES
    width = tokens.shape[1]
    event_type = event_type.reshape(1, -1)
    plane = lax.div(lax.axis_index("seq"), jnp.int32(owners)).reshape(1)

    def moved(x, to):
        return lax.ppermute(x, "seq", [(i, to(i)) for i in range(seq)])

    def to_plane(x, shift):
        return moved(x, lambda i: (i + shift * owners) % seq)

    def to_pair(x, shift):
        return moved(x, lambda i: i // owners * owners + (i % owners + CORES * shift) % owners)

    def to_core(x):
        return moved(x, lambda i: i ^ 1)

    packed = pl.pallas_call(
        pack_kernel,
        in_specs=[SMEM, HBM, HBM, VMEM, HBM],
        out_shape=[jax.ShapeDtypeStruct((PAIR, width // 2), BF16)] * TYPES,
        scratch_shapes=[
            pltpu.VMEM(tokens.shape, BF16),
            pltpu.VMEM(grad_out.shape, BF16),
            pltpu.VMEM(type_gain.shape, F32),
            pltpu.SemaphoreType.DMA((3,)),
        ],
        compiler_params=params(0, 0, 60 << 20),
    )(plane, tokens, grad_out, event_type, type_gain)
    acts, pres, norms, grads, gain_parts, returned = [], [], [], [], [], {}

    def work(rows, cross, after):
        normed, grad, act, pre = forward(rows + cross, up_weight, down_turned, after)
        acts.append(act)
        pres.append(pre)
        norms.append(normed)
        grads.append(grad)
        return pre, normed

    def leave(pre, normed, shifts, after, haste=HASTE):
        keep, send, gain = backward(pre, up_weight, normed, shifts, pairs, after, haste)
        gain_parts.append(gain)
        return keep, [to_core(x) for x in send[::-1]][::-1]

    def over_cores(kept, after):
        keep, got = kept
        sent = [merged(keep[j], got[j], after) for j in range(1, pairs)]
        return [keep[0], got[0]] + [to_pair(sent[j - 1], pairs - j) for j in range(1, pairs)], sent

    def over_planes(shifts, parts, after):
        sums = totals(parts, len(shifts), after)
        for shift, total in zip(shifts, sums):
            returned[shift] = to_plane(total, TYPES - shift) if shift else total
        return list(sums)[:1]

    def spread(x, after):
        row = [x] + [gated(to_pair(x, j), after) for j in range(1, pairs)]
        return row, [to_core(y) for y in row]

    down_turned = turned(down_weight, packed[0])
    one, two = to_plane(packed[1], 1), to_plane(packed[2], 2)
    warm = warmed(up_weight, down_turned, packed[0])
    row0, cross0 = spread(packed[0], [warm])
    row1, cross1 = spread(one, [warm])
    two = gated(two, [warm])
    last = gated(packed[3], [two])
    three = to_plane(last, 3)
    pre1, normed1 = work(row0 + row1, cross0 + cross1, [last])
    row2, cross2 = spread(two, [pre1])
    three = gated(three, [pre1])
    kept1 = leave(pre1, normed1, 2, row2[1:] + [three], 1)
    pre2, normed2 = work(row2, cross2, [gain_parts[0]])
    row3, cross3 = spread(three, [pre2])
    parts1, sent1 = over_cores(kept1, [pre2])
    kept2 = leave(pre2, normed2, 1, row3[1:] + sent1)
    pre3, normed3 = work(row3, cross3, [gain_parts[1]])
    parts2, sent2 = over_cores(kept2, [pre3])
    kept3 = leave(pre3, normed3, 1, sent2)
    total1 = over_planes((0, 1), parts1, [gain_parts[2]])
    total2 = over_planes((2,), parts2, total1)
    gain = summed(gain_parts, total2)
    gain = summed([gain, to_core(gain)], [])
    gain = summed([gain] + [to_pair(gain, j) for j in range(1, pairs)], [])
    gains = [gain] + [to_plane(gain, shift) for shift in range(1, TYPES)]
    tiles = max(2, width // 512)
    split = TILES_FIRST
    grad_up, done = weight_grad(norms, pres, total2, 0, split)
    parts3, sent3 = over_cores(kept3, [done])
    grad_up, done = weight_grad(norms, pres, sent3 + [returned[1]], split, tiles - split, grad_up)
    total3 = over_planes((3,), parts3, [done])
    grad_down, done = weight_grad(acts, grads, total3 + [returned[2]])
    grad_tokens, grad_gain = pl.pallas_call(
        finish_kernel,
        in_specs=[SMEM] + [VMEM] * (4 + 2 * TYPES),
        out_shape=[
            jax.ShapeDtypeStruct(tokens.shape, BF16),
            jax.ShapeDtypeStruct((TYPES, width), F32),
        ],
        compiler_params=params(2 * tokens.shape[0]),
    )(plane, tokens, grad_out, event_type, type_gain, *[returned[shift] for shift in range(TYPES)], *gains)
    return (grad_tokens, grad_gain, grad_up, grad_down)


def solution(mesh):
    placed = (
        P(("groups", "seq"), None),
        P(("groups", "seq"), None),
        P(("groups", "seq"), None),
        P(),
        P(None, "seq"),
        P("seq", None),
    )
    return jax.shard_map(
        local,
        mesh=mesh,
        in_specs=placed,
        out_specs=(
            P(("groups", "seq"), None),
            P("groups", None),
            P("groups", "seq"),
            P(("groups", "seq"), None),
        ),
        check_vma=False,
    )
```
